128 devices in a mesh: dp: 4 (over z), ctx: 32 (over y, x, core).
Axes of the slice: x: 4, y: 4, z: 4, core: 2. Of those that a mesh axis runs over, the one named last changes fastest.
Arguments:
- queries: bfloat16 [4, 4096, 1024], P('dp', 'ctx'), may hold values from -6 to 6
- key_in: bfloat16 [4, 4096, 1024], P('dp', 'ctx'), may hold values from -6 to 6
- value_in: bfloat16 [4, 4096, 2048], P('dp', 'ctx'), may hold values from -6 to 6
- gate_in: bfloat16 [4, 4096, 2048], P('dp', 'ctx'), may hold values from -6 to 6
- residual_in: bfloat16 [4, 4096, 2048], P('dp', 'ctx'), may hold values from -6 to 6
- log_decay: float32 [4, 16, 4096], P('dp', None, 'ctx'), may hold values from -1 to 0
- beta_logit: float32 [4, 16, 4096], P('dp', None, 'ctx'), may hold values from -6 to 6
- lengths: int32 [4, 4], P('dp'), may hold values from 1 to 2048, 4096 in all within a row
- head_gain: float32 [128], replicated, may hold values from 0.1 to 1.9
- out_proj: bfloat16 [2048, 2048], replicated, may hold values from -0.125 to 0.125
- post_gain: float32 [2048], replicated, may hold values from 0.1 to 1.9
- expert_in: bfloat16 [256, 2048, 1024], P(('dp', 'ctx')), may hold values from -0.125 to 0.125
- expert_out: bfloat16 [256, 512, 2048], P(('dp', 'ctx')), may hold values from -0.25 to 0.25
- routes: int32 [4, 4096, 10], P('dp', 'ctx'), may hold values from 0 to 255, all different within a row; in each aligned block of 128 rows (0 to 127, 128 to 255, ..., all dimensions but the last counted through in order) at most 6 rows name the same one
- route_gates: float32 [4, 4096, 10], P('dp', 'ctx'), may hold values from 0.05 to 0.25
Outputs:
- layer_out: bfloat16 [4, 4096, 2048], P('dp', 'ctx')
The draws below stay inside these ranges and needn't reach their ends.
Inputs may be any that keep to these rules, and one draw needn't show every extreme that they name: `routes`: each row names 10 different experts; among the rows of one device (aligned blocks of 128 positions) no expert is named more than 6 times, a bound that some block reaches. The lengths of a pack sum to 4096.
All inputs are finite; a program needn't handle non-finite values.
Results may differ from the reference program's by a relative error of at most 0.014.
Values may be sent and summed in bfloat16 or wider, within the bound.
No kernel may reach another device: no remote copies, remote signals or barrier semaphores. Data moves between devices by JAX's collectives and lax.ppermute only.
A program may use at most 256 MiB of HBM per device.

```python
import math
import jax
import jax.numpy as jnp
import numpy as np
from jax import lax

D = 2048
DK = 128
DV = 128
FF = 512
TOPK = 10
HK = 8
HV = 16
BLOCK = 64
NDOC = 4
TOK_DEV = 128
PACK_POSITIONS = 4096
PACKS = 4
EXPERTS = 256
CAP = 6
N_DP = 4
N_CTX = 32


def draw_log_decay(key, part):
    key = jax.random.fold_in(key, 7)
    variety_option_key, rate_option_key, jitter_option_key, block_option_key, spike_option_key, depth_option_key = jax.random.split(key, 6)
    tensor_extent = (PACKS, HV, PACK_POSITIONS)
    fast_share = 0.5
    fast_head = jax.random.uniform(variety_option_key, (PACKS, HV, 1)) < fast_share
    spread = jnp.exp(jax.random.uniform(rate_option_key, (PACKS, HV, 1), minval=0.0, maxval=math.log(2.0)))
    baseline_rate = jnp.where(fast_head, 1.0 / 40.0, 0.5 * math.log(10.0) / PACK_POSITIONS) * spread
    block_count = PACK_POSITIONS // TOK_DEV
    block_multiplier = jnp.exp(jax.random.uniform(block_option_key, (PACKS, HV, block_count, 1), minval=0.0, maxval=math.log(2.0)))
    block_multiplier = jnp.broadcast_to(block_multiplier, (PACKS, HV, block_count, TOK_DEV)).reshape(tensor_extent)
    jitter_level = jnp.exp(jax.random.uniform(jitter_option_key, tensor_extent, minval=math.log(0.5), maxval=math.log(1.5)))
    spike_train = jax.random.uniform(spike_option_key, tensor_extent) < 3.0 / PACK_POSITIONS
    spike_depth = jax.random.uniform(depth_option_key, tensor_extent, minval=0.22, maxval=0.69)
    return -(baseline_rate * block_multiplier * jitter_level) - jnp.where(spike_train, spike_depth, 0.0)


def block_levels(rng, extent, pieces, smallest, high):
    factor_of = 1.0
    for axis_at, parts in pieces:
        draws = jax.random.uniform(jax.random.fold_in(jax.random.fold_in(rng, 6), axis_at), (parts,), jnp.float32, smallest / len(pieces), high / len(pieces))
        factor_of = factor_of * jnp.repeat(jnp.exp(draws), extent[axis_at] // parts).reshape((-1,) + (1,) * (len(extent) - 1 - axis_at))
    return factor_of


def split_up(number_of, total, limit, lean):
    weights = [(1 << 20) // math.isqrt(rank ** lean) + 1 for rank in range(2, number_of + 1)]
    rest, counts = total - limit - (number_of - 1), [1] * (number_of - 1)
    while rest > 0:
        free = [i for i in range(number_of - 1) if counts[i] < limit]
        mass, left = sum([weights[i] for i in free]), rest
        for i in free:
            more = min(limit - counts[i], max(1, left * weights[i] // mass), rest)
            counts[i] = counts[i] + more
            rest = rest - more
    return np.array([limit] + counts)


def uneven_parts(own_key, amount, total, reach, lean):
    if amount == 2:
        one = jax.random.randint(own_key, (), max(1, total - reach), min(reach, total - 1) + 1)
        return jnp.stack([one, total - one])
    tallies = jnp.asarray(split_up(amount, total, reach, lean), jnp.int32)
    pairs = (amount - 1) // 2
    giver, sink = tallies[1:1 + 2 * pairs:2], tallies[2:2 + 2 * pairs:2]
    slack = jnp.minimum(giver - 1, reach - sink)
    moved = jax.random.randint(jax.random.fold_in(own_key, 1), (pairs,), 0, 1 << 20) % (slack + 1)
    tallies = tallies.at[1:1 + 2 * pairs:2].set(giver - moved).at[2:2 + 2 * pairs:2].set(sink + moved)
    return tallies[jax.random.permutation(jax.random.fold_in(own_key, 2), amount)]


def routed_block(rng, own, number, rows, number_of, top, most, slope):
    order = jax.random.permutation(rng, number_of)
    heavy_load, ordinary = portions_of(number_of, rows * top, most, slope, True), portions_of(number_of, rows * top, most, slope, False)
    places = jnp.arange(number_of)

    def named(sizes, offset_by):
        used = int((sizes > 0).sum())
        fixed = max(1, used // 4)
        passed = fixed + (places - fixed + offset_by * (used - fixed)) % max(1, number_of - fixed)
        return jnp.zeros((number_of,), jnp.int32).at[order[jnp.where(places < fixed, places, passed)]].set(jnp.asarray(sizes, jnp.int32))

    sizes = jnp.where(number % 4 == 0, named(heavy_load, number // 4), named(ordinary, number - number // 4 - 1))
    mixed = jax.random.permutation(jax.random.fold_in(own, 3), number_of)
    source_of, taker = mixed[0:number_of // 2 * 2:2], mixed[1:number_of // 2 * 2:2]
    room = jnp.minimum(sizes[source_of] - 1, most - sizes[taker]) // 2
    room = jnp.where((source_of == order[0]) | (taker == order[0]) | (sizes[taker] == 0), 0, jnp.maximum(room, 0))
    passed = jax.random.randint(jax.random.fold_in(own, 4), (number_of // 2,), 0, 1 << 20) % (room + 1)
    sizes = sizes.at[source_of].add(-passed).at[taker].add(passed)
    members = jnp.searchsorted(jnp.cumsum(sizes), jnp.arange(rows * top), side="right").astype(jnp.int32)
    grid = members.reshape(top, rows).T
    grid = grid[jax.random.permutation(jax.random.fold_in(own, 1), rows)]
    offset_by = jax.random.randint(jax.random.fold_in(own, 2), (rows, 1), 0, top)
    return jnp.take_along_axis(grid, (jnp.arange(top)[None, :] + offset_by) % top, axis=1)


def portions_of(count, total, limit, lean, full):
    loads = [(1 << 20) // math.isqrt(standing ** lean) + 1 for standing in range(1, count + 1)]
    largest = limit if full else min(limit, max(-(-total // count), total * loads[0] // sum(loads)))
    least = 1 if total - largest >= count - 1 else 0
    given, spare = [largest] + [least] * (count - 1), total - largest - least * (count - 1)
    while spare > 0:
        free = [i for i in range(1, count) if given[i] < largest] or [i for i in range(1, count) if given[i] < limit]
        pool, left = sum([loads[i] for i in free]), spare
        for i in free:
            extra = min(limit - given[i], max(1, left * loads[i] // pool), spare)
            given[i] = given[i] + extra
            spare = spare - extra
    return np.array(given)


def normal_values(own_key, extent, width, most, cuts=(), kind=jnp.bfloat16):
    values = width * jax.random.normal(own_key, extent, jnp.float32)
    if cuts:
        values = values * block_levels(own_key, extent, cuts, -0.22, 0.18)
    return jnp.clip(values, -most, most).astype(kind)


def setup_inputs(seed: int = 0) -> dict:
    streams_of = jax.random.split(jax.random.key(seed), 16)
    queries = normal_values(streams_of[0], (PACKS, PACK_POSITIONS, HK * DK), 1.0, 6.0, ((0, 4), (1, 32)))
    key_in = normal_values(streams_of[1], (PACKS, PACK_POSITIONS, HK * DK), 1.0, 6.0, ((0, 4), (1, 32)))
    value_in = normal_values(streams_of[2], (PACKS, PACK_POSITIONS, HV * DV), 1.0, 6.0, ((0, 4), (1, 32)))
    gate_in = normal_values(streams_of[3], (PACKS, PACK_POSITIONS, HV * DV), 1.0, 6.0, ((0, 4), (1, 32)))
    residual_in = normal_values(streams_of[4], (PACKS, PACK_POSITIONS, D), 1.0, 6.0, ((0, 4), (1, 32)))
    log_decay = draw_log_decay(jax.random.fold_in(streams_of[15], 71), 0)
    beta_logit = normal_values(streams_of[6], (PACKS, HV, PACK_POSITIONS), 1.5, 6.0, ((0, 4), (2, 32)), jnp.float32)
    lengths = jax.vmap(lambda own: uneven_parts(own, NDOC, PACK_POSITIONS, PACK_POSITIONS // 2, 2))(jax.random.split(streams_of[7], PACKS)).reshape((PACKS, NDOC)).astype(jnp.int32)
    head_gain = jnp.clip(1.0 + 0.18 * jax.random.normal(streams_of[8], (DV,), jnp.float32), 0.1, 1.9)
    out_proj = normal_values(streams_of[9], (HV * DV, D), (HV * DV) ** -0.5, 0.125)
    post_gain = jnp.clip(1.0 + 0.18 * jax.random.normal(streams_of[10], (D,), jnp.float32), 0.1, 1.9)
    expert_in = normal_values(streams_of[11], (EXPERTS, D, 2 * FF), D ** -0.5, 0.125, ((0, 128),))
    expert_out = normal_values(streams_of[12], (EXPERTS, FF, D), FF ** -0.5, 0.25, ((0, 128),))
    routes_keys = jax.random.split(jax.random.fold_in(streams_of[13], 1), PACKS * PACK_POSITIONS // TOK_DEV)
    routes_turns = jax.random.permutation(jax.random.fold_in(streams_of[13], 3), PACKS * PACK_POSITIONS // TOK_DEV)
    routes = jax.vmap(lambda own, number: routed_block(jax.random.fold_in(streams_of[13], 2), own, number, TOK_DEV, EXPERTS, TOPK, CAP, 2))(routes_keys, routes_turns).reshape((PACKS, PACK_POSITIONS, TOPK))
    route_gates = jnp.clip(0.05 + 0.2 * jax.random.uniform(streams_of[14], (PACKS, PACK_POSITIONS, TOPK), jnp.float32) ** block_levels(streams_of[14], (PACKS, PACK_POSITIONS, TOPK), ((0, 4), (1, 32)), -0.2, 0.2), 0.05, 0.25)
    return dict(queries=queries, key_in=key_in, value_in=value_in, gate_in=gate_in, residual_in=residual_in, log_decay=log_decay, beta_logit=beta_logit, lengths=lengths, head_gain=head_gain, out_proj=out_proj, post_gain=post_gain, expert_in=expert_in, expert_out=expert_out, routes=routes, route_gates=route_gates)


EPSILON = 1e-06
HIGHEST = lax.Precision.HIGHEST
ROWWISE = lax.Precision.HIGH

def unit_heads(matrix, head_count, factor):
    shaped = matrix.astype(jnp.float32).reshape(matrix.shape[0], head_count, -1)
    return shaped * lax.rsqrt(lax.optimization_barrier(jnp.sum(shaped * shaped, -1, keepdims=True)) + EPSILON) * factor

def segment_of(lengths, positions):
    starts = jnp.cumsum(lengths) - lengths
    return lax.optimization_barrier(jnp.sum((starts[:, None] <= positions[None, :]).astype(jnp.int32), 0)) - 1

def block_terms(queries, key_rows, value_rows, beta_gate, decay_log, segment, seg_before):
    length = key_rows.shape[1]
    cumulative = jnp.cumsum(decay_log, axis=-1)
    rows_at = jnp.arange(length)[:, None]
    cols_at = jnp.arange(length)[None, :]
    same_doc = (segment[:, None] == segment[None, :]) & (rows_at >= cols_at)
    log_gap = jnp.minimum(cumulative[:, :, None] - cumulative[:, None, :], 0.0)
    decay_pair = jnp.where(same_doc[None], jnp.exp(log_gap), 0.0)
    from_start = jnp.where((segment == seg_before)[None, :], jnp.exp(cumulative), 0.0)
    to_end = decay_pair[:, -1, :]
    key_inner = jnp.einsum('hcd,hsd->hcs', key_rows, key_rows, precision=ROWWISE)
    lower_part = jnp.where((rows_at > cols_at)[None], beta_gate[:, :, None] * decay_pair * key_inner, 0.0)
    system = jnp.eye(length, dtype=jnp.float32)[None] + lower_part
    right_side = jnp.concatenate([beta_gate[:, :, None] * value_rows, (beta_gate * from_start)[:, :, None] * key_rows], axis=-1)
    solved = jax.scipy.linalg.solve_triangular(system, right_side, lower=True, unit_diagonal=True)
    value_width = value_rows.shape[-1]
    pseudo = solved[..., :value_width]
    weights = solved[..., value_width:]
    scores = jnp.einsum('hcd,hsd->hcs', queries, key_rows, precision=ROWWISE) * decay_pair
    weighted = key_rows * to_end[:, :, None]
    key_width = key_rows.shape[-1]
    transition = from_start[:, -1][:, None, None] * jnp.eye(key_width, dtype=jnp.float32)[None] - jnp.einsum('hcd,hce->hde', weighted, weights, precision=HIGHEST)
    offset = jnp.einsum('hcd,hce->hde', weighted, pseudo, precision=HIGHEST)
    return (pseudo, weights, scores, from_start, transition, offset)

def block_output(queries, pseudo, weights, scores, from_start, carried):
    errors = pseudo - jnp.einsum('hcd,hde->hce', weights, carried, precision=ROWWISE)
    return jnp.einsum('hcd,hde->hce', queries * from_start[:, :, None], carried, precision=ROWWISE) + jnp.einsum('hcs,hse->hce', scores, errors, precision=ROWWISE)

def apply_map(transition, carried):
    return jnp.einsum('hde,hef->hdf', transition, carried, precision=HIGHEST)

def head_blocks(matrix, block_len):
    length, head_count, inner_width = matrix.shape
    return matrix.reshape(length // block_len, block_len, head_count, inner_width).transpose(0, 2, 1, 3)

def prepare(queries, key_in, value_in, log_decay, beta_logit, segment, seg_before):
    length = queries.shape[0]
    group_size = HV // HK
    query_heads = jnp.repeat(unit_heads(queries, HK, DK ** (-0.5)), group_size, axis=1)
    key_heads = jnp.repeat(unit_heads(key_in, HK, 1.0), group_size, axis=1)
    value_heads = value_in.astype(jnp.float32).reshape(length, HV, DV)
    nblock = length // BLOCK
    beta_gate = jax.nn.sigmoid(beta_logit).reshape(HV, nblock, BLOCK).transpose(1, 0, 2)
    decay_log = log_decay.reshape(HV, nblock, BLOCK).transpose(1, 0, 2)
    seg_blocks = segment.reshape(nblock, BLOCK)
    seg_starts = jnp.concatenate([jnp.reshape(seg_before, (1,)).astype(jnp.int32), seg_blocks[:-1, -1]])
    query_blocks = head_blocks(query_heads, BLOCK)
    terms = jax.vmap(block_terms)(query_blocks, head_blocks(key_heads, BLOCK), head_blocks(value_heads, BLOCK), beta_gate, decay_log, seg_blocks, seg_starts)
    return (query_blocks, terms)

def finish(query_blocks, terms, start_state, gate_in, residual_in, head_gain, out_proj):
    pseudo, weights, scores, from_start, transition, offset = terms

    def advance(carried, member):
        return (apply_map(member[0], carried) + member[1], carried)
    final_state, block_starts = lax.scan(advance, start_state, (transition, offset))
    outputs = jax.vmap(block_output)(query_blocks, pseudo, weights, scores, from_start, block_starts)
    length = gate_in.shape[0]
    outputs = outputs.transpose(0, 2, 1, 3).reshape(length, HV, DV)
    mean_square = lax.optimization_barrier(jnp.mean(outputs * outputs, -1, keepdims=True))
    gate_heads = gate_in.astype(jnp.float32).reshape(length, HV, DV)
    normed = (outputs * lax.rsqrt(mean_square + EPSILON) * head_gain * jax.nn.silu(gate_heads)).reshape(length, HV * DV).astype(jnp.bfloat16)
    mixed = jnp.dot(normed.astype(jnp.float32), out_proj.astype(jnp.float32), preferred_element_type=jnp.float32)
    return (residual_in.astype(jnp.float32) + mixed).astype(jnp.bfloat16)

def post_norm(hidden_state, post_gain):
    widened = hidden_state.astype(jnp.float32)
    return (widened * lax.rsqrt(lax.optimization_barrier(jnp.mean(widened * widened, -1, keepdims=True)) + EPSILON) * post_gain).astype(jnp.bfloat16)

def rank_of(flat_ids, experts):
    onehot = (flat_ids[:, None] == jnp.arange(experts, dtype=jnp.int32)[None, :]).astype(jnp.int32)
    return lax.optimization_barrier(jnp.sum((jnp.cumsum(onehot, 0) - onehot) * onehot, 1))

def reference(queries, key_in, value_in, gate_in, residual_in, log_decay, beta_logit, lengths, head_gain, out_proj, post_gain, expert_in, expert_out, routes, route_gates):
    positions = jnp.arange(PACK_POSITIONS, dtype=jnp.int32)

    def one_pack(pack_args):
        pack_query, pack_keys, pack_values, pack_gates, pack_resid, pack_decay, pack_beta, pack_lengths = pack_args
        segment = segment_of(pack_lengths, positions)
        query_blocks, terms = prepare(pack_query, pack_keys, pack_values, pack_decay, pack_beta, segment, jnp.array(-1, jnp.int32))
        zero_state = jnp.zeros((HV, DK, DV), jnp.float32)
        return finish(query_blocks, terms, zero_state, pack_gates, pack_resid, head_gain, out_proj)
    hidden_state = lax.map(one_pack, (queries, key_in, value_in, gate_in, residual_in, log_decay, beta_logit, lengths))
    blocks = N_DP * N_CTX
    expert_input = post_norm(hidden_state, post_gain).reshape(blocks, TOK_DEV, D)
    flat_ids = routes.reshape(blocks, TOK_DEV * TOPK)

    def block_rank(block_ids):
        return rank_of(block_ids, EXPERTS)
    slot_rank = jax.vmap(block_rank)(flat_ids)

    def fill_block(member):
        block_rows, block_ids, block_ranks = member
        return jnp.zeros((EXPERTS, CAP, D), jnp.bfloat16).at[block_ids, block_ranks].set(jnp.repeat(block_rows, TOPK, axis=0))
    buffers = lax.map(fill_block, (expert_input, flat_ids, slot_rank))

    def run_expert(expert_index):
        routed_rows = lax.dynamic_index_in_dim(buffers, expert_index, 1, keepdims=False).reshape(blocks * CAP, D)
        gate_up = jnp.dot(routed_rows.astype(jnp.float32), lax.dynamic_index_in_dim(expert_in, expert_index, 0, keepdims=False).astype(jnp.float32), preferred_element_type=jnp.float32)
        hidden_units = (jax.nn.silu(gate_up[:, :FF]) * gate_up[:, FF:]).astype(jnp.bfloat16)
        result = jnp.dot(hidden_units.astype(jnp.float32), lax.dynamic_index_in_dim(expert_out, expert_index, 0, keepdims=False).astype(jnp.float32), preferred_element_type=jnp.float32)
        return result.astype(jnp.bfloat16).reshape(blocks, CAP, D)
    results = lax.map(run_expert, jnp.arange(EXPERTS, dtype=jnp.int32))

    def gather_back(member):
        block_index, block_ids, block_ranks, block_gates = member
        picked = results[block_ids, block_index, block_ranks].astype(jnp.float32).reshape(TOK_DEV, TOPK, D)
        return lax.optimization_barrier(jnp.sum(picked * block_gates[:, :, None], 1))
    expert_mix = lax.map(gather_back, (jnp.arange(blocks, dtype=jnp.int32), flat_ids, slot_rank, route_gates.reshape(blocks, TOK_DEV, TOPK)))
    summed = hidden_state.reshape(blocks, TOK_DEV, D).astype(jnp.float32) + expert_mix
    return summed.reshape(PACKS, PACK_POSITIONS, D).astype(jnp.bfloat16)
```

```python
import functools

import jax
import jax.numpy as jnp
from jax import lax
from jax.experimental import pallas as pl
from jax.experimental.pallas import tpu as pltpu
from jax.sharding import PartitionSpec as P

D = 2048
DK = 128
DV = 128
FF = 512
TOPK = 10
HK = 8
HV = 16
TOK = 128
CAP = 6
GROUPS = 4
WIDTH = D // GROUPS
SPAN = GROUPS * CAP
EPSILON = 1e-06

F32 = jnp.float32
BF16 = jnp.bfloat16
HEADS_STEP = 8
MAP_ROWS = 64 + 128 + 16
SRC_GROUP = 8
GROUP_ROWS = SRC_GROUP * SPAN
PIECE = SRC_GROUP * CAP
MIB = 1 << 20


def dot_nn(a, b):
    return lax.dot_general(a, b, (((1,), (0,)), ((), ())), preferred_element_type=F32)


def dot_nt(a, b):
    return lax.dot_general(a, b, (((1,), (1,)), ((), ())), preferred_element_type=F32)


def halves(x):
    high = x.astype(BF16)
    return high, (x - high.astype(F32)).astype(BF16)


def wide(x):
    high, low = halves(x)
    return jnp.concatenate([high, low], axis=1)


def twice(x, axis):
    return jnp.concatenate([x, x], axis=axis)


def iota(shape, axis):
    return lax.broadcasted_iota(jnp.int32, shape, axis)


def params(limit=48 * MIB):
    return pltpu.CompilerParams(vmem_limit_bytes=limit)


def mixer_kernel(
    len_ref, q_ref, k_ref, v_ref, decay_ref, beta_ref, maps_ref, query_ref, local_ref
):
    first = lax.axis_index("ctx") * TOK
    start1 = len_ref[0, 0]
    start2 = start1 + len_ref[0, 1]
    start3 = start2 + len_ref[0, 2]

    def segment(at):
        return (
            (at >= 0).astype(jnp.int32)
            + (at >= start1).astype(jnp.int32)
            + (at >= start2).astype(jnp.int32)
            + (at >= start3).astype(jnp.int32)
        )

    square = (TOK, TOK)
    rows, cols = iota(square, 0), iota(square, 1)
    seg_rows, seg_cols = segment(first + rows), segment(first + cols)
    seg_before, seg_last = segment(first - 1), segment(first + TOK - 1)
    lower = (seg_rows == seg_cols) & (rows >= cols)
    strict = rows > cols
    diagonal = rows == cols
    eye = diagonal.astype(F32)
    eye_bf = eye.astype(BF16)
    pair_masks = {}
    size = 1
    while size < TOK:
        pair_masks[size] = (rows // (2 * size) == cols // (2 * size)) & (
            rows // size != cols // size
        )
        size *= 2

    heads = range(HEADS_STEP)
    keys = range(HEADS_STEP // 2)
    upper = (rows <= cols).astype(F32)
    cum_row = lax.dot_general(
        decay_ref[...],
        upper,
        (((1,), (0,)), ((), ())),
        precision=lax.Precision.HIGHEST,
        preferred_element_type=F32,
    )
    beta_row = 1.0 / (1.0 + jnp.exp(-beta_ref[...]))
    columns = jnp.concatenate(
        [cum_row, beta_row, jnp.zeros((TOK - 2 * HEADS_STEP, TOK), F32)], axis=0
    ).T
    row8 = iota((HEADS_STEP, TOK), 1)
    enter_row = jnp.where(segment(first + row8) == seg_before, jnp.exp(cum_row), 0.0)
    col_at = iota((TOK, 1), 0)
    enters = segment(first + col_at) == seg_before
    leaves = segment(first + col_at) == seg_last

    key = [k_ref[:, i * DK : (i + 1) * DK] for i in keys]
    query = [q_ref[:, i * DK : (i + 1) * DK] for i in keys]
    key_t = [k.T for k in key]
    inner = [dot_nt(k, k) for k in key]
    cross = [dot_nt(q, k) for q, k in zip(query, key)]
    inner_diag = [jnp.where(diagonal, x, 0.0) for x in inner]
    key_row = [lax.rsqrt(jnp.sum(x, 0, keepdims=True) + EPSILON) for x in inner_diag]
    key_col = [lax.rsqrt(jnp.sum(x, 1, keepdims=True) + EPSILON) for x in inner_diag]
    query_f = [q.astype(F32) for q in query]
    query_col = [
        lax.rsqrt(jnp.sum(q * q, 1, keepdims=True) + EPSILON) * (DK**-0.5) for q in query_f
    ]
    inner = [x * r for x, r in zip(inner, key_row)]
    cross = [x * r * c for x, r, c in zip(cross, key_row, query_col)]

    cum_col = [columns[:, h : h + 1] for h in heads]
    beta_col = [columns[:, HEADS_STEP + h : HEADS_STEP + h + 1] for h in heads]
    decay = [
        jnp.where(lower, jnp.exp(jnp.minimum(cum_col[h] - cum_row[h : h + 1], 0.0)), 0.0)
        for h in heads
    ]
    system = [
        jnp.where(strict, (beta_col[h] * key_col[h // 2]) * decay[h] * inner[h // 2], 0.0)
        for h in heads
    ]
    system_bf = [x.astype(BF16) for x in system]
    zero_bf = jnp.zeros(square, BF16)
    inverse = [eye_bf - jnp.where(pair_masks[1], x, zero_bf) for x in system_bf]
    size = 2
    while size < TOK:
        mask = pair_masks[size]
        inside = [
            dot_nn(jnp.where(mask, system_bf[h], zero_bf), inverse[h]).astype(BF16) for h in heads
        ]
        inverse = [inverse[h] - dot_nn(inverse[h], inside[h]).astype(BF16) for h in heads]
        size *= 2
    residual = [
        (eye - inverse[h].astype(F32) - dot_nn(wide(system[h]), twice(inverse[h], 0))).astype(BF16)
        for h in heads
    ]
    solve = [inverse[h].astype(F32) + dot_nn(inverse[h], residual[h]) for h in heads]

    key_pair = [twice(k, 0) for k in key]
    key_t_pair = [twice(k, 1) for k in key_t]
    value = [v_ref[:, h * DV : (h + 1) * DV] for h in heads]
    weight_row = [beta_row[h : h + 1] * enter_row[h : h + 1] * key_row[h // 2] for h in heads]
    leave_col = [
        jnp.where(leaves, jnp.exp(jnp.minimum(cum_col[h][TOK - 1 :] - cum_col[h], 0.0)), 0.0)
        * key_col[h // 2]
        for h in heads
    ]
    left = [leave_col[h] * solve[h] for h in heads]
    offset_in = [
        dot_nt(twice(value[h].T, 1), wide(left[h] * beta_row[h : h + 1])) for h in heads
    ]
    change_in = [dot_nt(key_t_pair[h // 2], wide(left[h] * weight_row[h])) for h in heads]
    offset = [dot_nn(wide(offset_in[h]), key_pair[h // 2]).astype(BF16) for h in heads]
    change = [dot_nn(wide(change_in[h]), key_pair[h // 2]).astype(BF16) for h in heads]
    at_row = iota((16, TOK), 0)
    for h in heads:
        keep = jnp.broadcast_to(enter_row[h : h + 1, TOK - 1 :], (16, TOK))
        keep_high = keep.astype(BF16)
        keep_mid, keep_low = halves(keep - keep_high.astype(F32))
        terms = jnp.where(
            at_row == 0,
            keep_high.astype(F32),
            jnp.where(
                at_row == 1,
                keep_mid.astype(F32),
                jnp.where(at_row == 2, keep_low.astype(F32), 0.0),
            ),
        ).astype(BF16)
        for s in range(2):
            maps_ref[2 * h + s, 0:64, :] = offset[h][s * 64 : (s + 1) * 64]
            maps_ref[2 * h + s, 64:192, :] = change[h]
            maps_ref[2 * h + s, 192:208, :] = terms

    mixed = []
    for h in heads:
        score_high, score_low = halves(decay[h] * cross[h // 2])
        solve_high, solve_low = halves(solve[h])
        mixed.append(
            dot_nn(
                jnp.concatenate([score_high, score_low, score_high], axis=1),
                jnp.concatenate([solve_high, solve_high, solve_low], axis=0),
            )
        )
    for h in heads:
        local_ref[:, h * DV : (h + 1) * DV] = dot_nn(
            wide(mixed[h] * beta_row[h : h + 1]), twice(value[h], 0)
        )
    for h in heads:
        enter_col = jnp.where(enters, jnp.exp(cum_col[h]), 0.0) * query_col[h // 2]
        query_ref[h] = enter_col * query_f[h // 2] - dot_nn(
            wide(mixed[h] * weight_row[h]), key_pair[h // 2]
        )


def mixer_call(lengths, queries, key_in, value_in, log_decay, beta_logit):
    steps = HV // HEADS_STEP
    return pl.pallas_call(
        mixer_kernel,
        grid=(steps,),
        in_specs=[
            pl.BlockSpec(memory_space=pltpu.SMEM),
            pl.BlockSpec((TOK, HK * DK // steps), lambda i: (0, i)),
            pl.BlockSpec((TOK, HK * DK // steps), lambda i: (0, i)),
            pl.BlockSpec((TOK, HV * DV // steps), lambda i: (0, i)),
            pl.BlockSpec((HEADS_STEP, TOK), lambda i: (i, 0)),
            pl.BlockSpec((HEADS_STEP, TOK), lambda i: (i, 0)),
        ],
        out_specs=[
            pl.BlockSpec((2 * HEADS_STEP, MAP_ROWS, DK), lambda i: (i, 0, 0)),
            pl.BlockSpec((HEADS_STEP, TOK, DK), lambda i: (i, 0, 0)),
            pl.BlockSpec((TOK, HV * DV // steps), lambda i: (0, i)),
        ],
        out_shape=[
            jax.ShapeDtypeStruct((2 * HV, MAP_ROWS, DK), BF16),
            jax.ShapeDtypeStruct((HV, TOK, DK), F32),
            jax.ShapeDtypeStruct((TOK, HV * DV), F32),
        ],
        compiler_params=params(),
        name="mixer_block",
    )(lengths, queries, key_in, value_in, log_decay, beta_logit)


def scan_kernel(maps_ref, out_ref):
    blocks = maps_ref.shape[0]
    state = jnp.zeros((64, DK), F32)
    for at in range(blocks):
        high, low = halves(state)
        out_ref[at * 64 : (at + 1) * 64, :] = high
        if at < blocks - 1:
            offset = maps_ref[at, 0:64, :].astype(F32)
            change = maps_ref[at, 64:192, :]
            keep = jnp.sum(maps_ref[at, 192:208, :].astype(F32), 0, keepdims=True)
            moved = dot_nn(jnp.concatenate([high, low], axis=0), change)
            state = keep * state - (moved[:64] + moved[64:]) + offset


def scan_call(maps):
    blocks = maps.shape[0]
    return pl.pallas_call(
        scan_kernel,
        out_shape=jax.ShapeDtypeStruct((blocks * 64, DK), BF16),
        compiler_params=params(),
        name="state_scan",
    )(maps)


def finish_kernel(
    state_ref,
    query_ref,
    local_ref,
    gate_ref,
    resid_ref,
    gain_ref,
    proj_ref,
    post_ref,
    hidden_ref,
    rows_ref,
):
    gain = gain_ref[...]
    normed = []
    for h in range(HV):
        cut = slice(h * DV, (h + 1) * DV)
        outputs = local_ref[:, cut] + dot_nt(wide(query_ref[h]), twice(state_ref[cut, :], 1))
        scale = lax.rsqrt(jnp.mean(outputs * outputs, -1, keepdims=True) + EPSILON)
        gate = gate_ref[:, cut].astype(F32)
        normed.append((outputs * scale * gain * (gate / (1.0 + jnp.exp(-gate)))).astype(BF16))
    normed = jnp.concatenate(normed, axis=1)
    total = jnp.zeros((TOK, 1), F32)
    parts = []
    for g in range(GROUPS):
        cut = slice(g * WIDTH, (g + 1) * WIDTH)
        hidden = (resid_ref[:, cut].astype(F32) + dot_nn(normed, proj_ref[:, cut])).astype(BF16)
        hidden_ref[:, cut] = hidden
        hidden = hidden.astype(F32)
        total = total + jnp.sum(hidden * hidden, -1, keepdims=True)
        parts.append(hidden)
    scale = lax.rsqrt(total / D + EPSILON)
    for g in range(GROUPS):
        cut = slice(g * WIDTH, (g + 1) * WIDTH)
        rows_ref[g * TOK : (g + 1) * TOK, :] = (parts[g] * scale * post_ref[:, cut]).astype(BF16)


def finish_call(state, query, local, gate_in, residual_in, head_gain, out_proj, post_gain):
    return pl.pallas_call(
        finish_kernel,
        out_shape=[
            jax.ShapeDtypeStruct((TOK, D), BF16),
            jax.ShapeDtypeStruct((GROUPS * TOK, WIDTH), BF16),
        ],
        compiler_params=params(),
        name="mixer_finish",
    )(state, query, local, gate_in, residual_in, head_gain, out_proj, post_gain)


def route_kernel(routes_ref, gates_ref, code_ref, code_t_ref, gate_ref):
    experts = code_ref.shape[1]
    half = experts // 2
    lane = iota((TOK, experts), 1)
    expert = jnp.where(lane < half, 2 * lane, 2 * (lane - half) + 1)
    hit = jnp.zeros((TOK, experts), F32)
    gate = jnp.zeros((TOK, experts), F32)
    for k in range(TOPK):
        match = routes_ref[:, k : k + 1] == expert
        hit = jnp.where(match, 1.0, hit)
        gate = jnp.where(match, gates_ref[:, k : k + 1], gate)
    square = (TOK, TOK)
    before = (iota(square, 0) > iota(square, 1)).astype(BF16)
    rank = dot_nn(before, hit.astype(BF16))
    code = jnp.where(hit > 0.0, rank, -1.0)
    code_ref[...] = code.astype(BF16)
    code_t_ref[0:half, :] = code[:, :half].T
    code_t_ref[half:, :] = code[:, half:].T
    high, low = halves(gate)
    gate_ref[0:TOK, :] = high
    gate_ref[TOK:, :] = low


def route_call(routes, gates, experts):
    return pl.pallas_call(
        route_kernel,
        out_shape=[
            jax.ShapeDtypeStruct((TOK, experts), BF16),
            jax.ShapeDtypeStruct((experts, TOK), F32),
            jax.ShapeDtypeStruct((2 * TOK, experts), BF16),
        ],
        compiler_params=params(),
        name="routing",
    )(routes, gates)


def dispatch_kernel(code_ref, rows_ref, out_ref):
    count = code_ref.shape[0]
    shape = (count, SPAN, TOK)
    at = iota(shape, 1)
    code = jnp.broadcast_to(code_ref[...][:, None, :], shape)
    match = code == (at % CAP).astype(F32)
    group = at // CAP
    pick = jnp.concatenate(
        [
            jnp.where(match & (group == g), 1.0, 0.0).reshape(count * SPAN, TOK).astype(BF16)
            for g in range(GROUPS)
        ],
        axis=1,
    )
    out_ref[...] = dot_nn(pick, rows_ref[...]).astype(BF16)


def dispatch_call(code_t, rows, local, devices):
    tile = 32
    steps = devices // tile
    return pl.pallas_call(
        dispatch_kernel,
        grid=(steps,),
        in_specs=[
            pl.BlockSpec((tile, TOK), lambda i: (local * steps + i, 0)),
            pl.BlockSpec((GROUPS * TOK, WIDTH), lambda i: (0, 0)),
        ],
        out_specs=pl.BlockSpec((tile * SPAN, WIDTH), lambda i: (i, 0)),
        out_shape=jax.ShapeDtypeStruct((devices * SPAN, WIDTH), BF16),
        compiler_params=params(),
        name="dispatch_rows",
    )(code_t, rows)


def expert_kernel(rows_ref, in_ref, out_ref, result_ref, x_ref, y_ref):
    count = rows_ref.shape[0] // GROUP_ROWS
    square = (GROUP_ROWS, GROUP_ROWS)
    to_at, from_at = iota(square, 0), iota(square, 1)

    def source_of(at):
        group, rest = at // PIECE, at % PIECE
        return (rest // CAP) * SPAN + group * CAP + rest % CAP

    order = (source_of(to_at) == from_at).astype(BF16)
    back = (source_of(from_at) == to_at).astype(BF16)
    for i in range(count):
        block = rows_ref[i * GROUP_ROWS : (i + 1) * GROUP_ROWS, :]
        moved = dot_nn(order, block).astype(BF16)
        for g in range(GROUPS):
            x_ref[i * PIECE : (i + 1) * PIECE, g * WIDTH : (g + 1) * WIDTH] = moved[
                g * PIECE : (g + 1) * PIECE
            ]
    x = x_ref[...]
    gate = dot_nn(x, in_ref[:, :FF])
    up = dot_nn(x, in_ref[:, FF:])
    hidden = (gate / (1.0 + jnp.exp(-gate)) * up).astype(BF16)
    y_ref[...] = dot_nn(hidden, out_ref[...]).astype(BF16)
    for i in range(count):
        block = jnp.concatenate(
            [
                y_ref[i * PIECE : (i + 1) * PIECE, g * WIDTH : (g + 1) * WIDTH]
                for g in range(GROUPS)
            ],
            axis=0,
        )
        result_ref[i * GROUP_ROWS : (i + 1) * GROUP_ROWS, :] = dot_nn(back, block).astype(BF16)


def expert_call(rows, expert_in, expert_out, local):
    total = rows.shape[0]
    steps = 2
    tile = total // steps
    tokens = tile // GROUPS
    return pl.pallas_call(
        expert_kernel,
        grid=(steps,),
        in_specs=[
            pl.BlockSpec((tile, WIDTH), lambda i: (i, 0)),
            pl.BlockSpec((None, D, 2 * FF), lambda i: (local, 0, 0)),
            pl.BlockSpec((None, FF, D), lambda i: (local, 0, 0)),
        ],
        out_specs=pl.BlockSpec((tile, WIDTH), lambda i: (i, 0)),
        out_shape=jax.ShapeDtypeStruct((total, WIDTH), BF16),
        scratch_shapes=[pltpu.VMEM((tokens, D), BF16), pltpu.VMEM((tokens, D), BF16)],
        compiler_params=params(),
        name="expert",
    )(rows, expert_in, expert_out)


def combine_kernel(code_ref, gate_ref, rows_ref, before_ref, *rest, last):
    if last:
        hidden_ref, out_ref, total_ref = rest
    else:
        out_ref, total_ref = rest
    step = pl.program_id(0)
    tile = rows_ref.shape[0]
    devices = code_ref.shape[1]
    spread_shape = (devices, tile)
    owner = (iota(spread_shape, 1) + step * tile) // SPAN
    spread = (owner == iota(spread_shape, 0)).astype(BF16)
    code = dot_nn(code_ref[...], spread)
    gate = dot_nn(gate_ref[...], spread).astype(BF16)
    at = iota((TOK, tile), 1) + step * tile
    match = code == (at % CAP).astype(F32)
    group = at // CAP % GROUPS
    zero = jnp.zeros((TOK, tile), BF16)
    weights = []
    for g in range(GROUPS):
        chosen = match & (group == g)
        weights.append(jnp.where(chosen, gate[:TOK], zero))
        weights.append(jnp.where(chosen, gate[TOK:], zero))
    part = dot_nn(jnp.concatenate(weights, axis=0), rows_ref[...])

    @pl.when(step == 0)
    def _():
        total_ref[...] = part

    @pl.when(step > 0)
    def _():
        total_ref[...] += part

    @pl.when(step == pl.num_programs(0) - 1)
    def _():
        for g in range(GROUPS):
            base = 2 * g * TOK
            mix = total_ref[base : base + TOK, :] + total_ref[base + TOK : base + 2 * TOK, :]
            cut = slice(g * WIDTH, (g + 1) * WIDTH)
            if last:
                out_ref[:, cut] = (
                    hidden_ref[:, cut].astype(F32) + (before_ref[:, cut] + mix)
                ).astype(BF16)
            else:
                out_ref[:, cut] = mix


def combine_call(code, gate, rows, local, before=None, hidden=None):
    total = rows.shape[0]
    steps = 4
    tile = total // steps
    devices = code.shape[1] // 2
    last = before is not None
    in_specs = [
        pl.BlockSpec((TOK, devices), lambda i: (0, local)),
        pl.BlockSpec((2 * TOK, devices), lambda i: (0, local)),
        pl.BlockSpec((tile, WIDTH), lambda i: (i, 0)),
    ]
    operands = [code, gate, rows]
    if last:
        in_specs += [pl.BlockSpec((TOK, D), lambda i: (0, 0))] * 2
        operands += [before, hidden]

    def body(code_ref, gate_ref, rows_ref, *rest):
        if last:
            combine_kernel(code_ref, gate_ref, rows_ref, *rest, last=True)
        else:
            combine_kernel(code_ref, gate_ref, rows_ref, None, *rest, last=False)

    return pl.pallas_call(
        body,
        grid=(steps,),
        in_specs=in_specs,
        out_specs=pl.BlockSpec((TOK, D), lambda i: (0, 0)),
        out_shape=jax.ShapeDtypeStruct((TOK, D), BF16 if last else F32),
        scratch_shapes=[pltpu.VMEM((2 * GROUPS * TOK, WIDTH), F32)],
        compiler_params=params(),
        name="combine_last" if last else "combine_first",
    )(*operands)


def exchange(rows, axes):
    return lax.all_to_all(rows, axes, split_axis=0, concat_axis=0, tiled=True)


def per_device(
    queries,
    key_in,
    value_in,
    gate_in,
    residual_in,
    log_decay,
    beta_logit,
    lengths,
    head_gain,
    out_proj,
    post_gain,
    expert_in,
    expert_out,
    routes,
    route_gates,
):
    devices = lax.axis_size("dp") * lax.axis_size("ctx")
    maps, query, local = mixer_call(
        lengths, queries[0], key_in[0], value_in[0], log_decay[0], beta_logit[0]
    )
    code, code_t, gate = route_call(routes[0], route_gates[0], 2 * devices)
    states = exchange(scan_call(exchange(maps, "ctx")), "ctx")
    hidden, rows = finish_call(
        states,
        query,
        local,
        gate_in[0],
        residual_in[0],
        head_gain[None],
        out_proj,
        post_gain[None],
    )
    both = ("dp", "ctx")

    def chunks(x):
        return x.reshape(devices, SPAN, WIDTH)

    def flat(x):
        return x.reshape(devices * SPAN, WIDTH)

    sent = [dispatch_call(code_t, rows, j, devices) for j in range(2)]
    arrived = [flat(exchange(chunks(x), both)) for x in sent]
    results = [expert_call(arrived[j], expert_in, expert_out, j) for j in range(2)]
    returned = [flat(exchange(chunks(x), both)) for x in results]
    first = combine_call(code, gate, returned[0], 0)
    return combine_call(code, gate, returned[1], 1, first, hidden)[None]


def solution(mesh):
    tokens = P("dp", "ctx", None)
    heads = P("dp", None, "ctx")
    experts = P(("dp", "ctx"), None, None)
    in_specs = (tokens,) * 5 + (heads, heads, P("dp", None), P(), P(), P())
    in_specs += (experts, experts, tokens, tokens)
    return jax.shard_map(
        per_device, mesh=mesh, in_specs=in_specs, out_specs=tokens, check_vma=False
    )
```

```python
import jax
import jax.numpy as jnp
from jax import lax
from jax.experimental import pallas as pl
from jax.experimental.pallas import tpu as pltpu
from jax.sharding import PartitionSpec as P

D = 2048
DK = 128
DV = 128
FF = 512
TOPK = 10
HK = 8
HV = 16
TOK = 128
CAP = 6
GROUPS = 4
WIDTH = D // GROUPS
SPAN = GROUPS * CAP
EPSILON = 1e-06

F32 = jnp.float32
BF16 = jnp.bfloat16
HEADS_STEP = 8
MAP_ROWS = 64 + 128 + 16
SRC_GROUP = 4
GROUP_ROWS = SRC_GROUP * SPAN
PIECE = SRC_GROUP * CAP
DISPATCH_STEPS = 8
MIB = 1 << 20


def dot_nn(a, b):
    return lax.dot_general(a, b, (((1,), (0,)), ((), ())), preferred_element_type=F32)


def dot_nt(a, b):
    return lax.dot_general(a, b, (((1,), (1,)), ((), ())), preferred_element_type=F32)


def halves(x):
    high = x.astype(BF16)
    return high, (x - high.astype(F32)).astype(BF16)


def wide(x):
    high, low = halves(x)
    return jnp.concatenate([high, low], axis=1)


def twice(x, axis):
    return jnp.concatenate([x, x], axis=axis)


def iota(shape, axis):
    return lax.broadcasted_iota(jnp.int32, shape, axis)


def params(limit=60 * MIB):
    return pltpu.CompilerParams(vmem_limit_bytes=limit)


def block_frame(len_ref, k_ref, decay_ref, beta_ref):
    first = lax.axis_index("ctx") * TOK
    start1 = len_ref[0, 0]
    start2 = start1 + len_ref[0, 1]
    start3 = start2 + len_ref[0, 2]

    def segment(at):
        return (
            (at >= 0).astype(jnp.int32)
            + (at >= start1).astype(jnp.int32)
            + (at >= start2).astype(jnp.int32)
            + (at >= start3).astype(jnp.int32)
        )

    square = (TOK, TOK)
    rows, cols = iota(square, 0), iota(square, 1)
    seg_before, seg_last = segment(first - 1), segment(first + TOK - 1)
    lower = (segment(first + rows) == segment(first + cols)) & (rows >= cols)
    cum_row = lax.dot_general(
        decay_ref[...],
        (rows <= cols).astype(F32),
        (((1,), (0,)), ((), ())),
        precision=lax.Precision.HIGHEST,
        preferred_element_type=F32,
    )
    beta_row = 1.0 / (1.0 + jnp.exp(-beta_ref[...]))
    columns = jnp.concatenate(
        [cum_row, beta_row, jnp.zeros((TOK - 2 * HEADS_STEP, TOK), F32)], axis=0
    ).T
    row8 = iota((HEADS_STEP, TOK), 1)
    enter_row = jnp.where(segment(first + row8) == seg_before, jnp.exp(cum_row), 0.0)
    at = first + iota((TOK, 1), 0)
    enters, leaves = segment(at) == seg_before, segment(at) == seg_last
    cum_col = [columns[:, h : h + 1] for h in range(HEADS_STEP)]
    beta_col = [columns[:, HEADS_STEP + h : HEADS_STEP + h + 1] for h in range(HEADS_STEP)]
    key = [k_ref[:, i * DK : (i + 1) * DK] for i in range(HEADS_STEP // 2)]
    inner = [dot_nt(k, k) for k in key]
    squares = [jnp.where(rows == cols, x, 0.0) for x in inner]
    key_row = [lax.rsqrt(jnp.sum(x, 0, keepdims=True) + EPSILON) for x in squares]
    key_col = [lax.rsqrt(jnp.sum(x, 1, keepdims=True) + EPSILON) for x in squares]
    decay = [
        jnp.where(
            lower, jnp.exp(jnp.minimum(cum_col[h] - cum_row[h : h + 1], 0.0)), 0.0
        )
        for h in range(HEADS_STEP)
    ]
    rows_of = (beta_row, enter_row, key_row)
    columns_of = (cum_col, beta_col, key_col, enters, leaves)
    return rows, cols, key, inner, decay, rows_of, columns_of


def maps_kernel(len_ref, k_ref, v_ref, decay_ref, beta_ref, maps_ref, solve_ref):
    rows, cols, key, inner, decay, rows_of, columns_of = block_frame(
        len_ref, k_ref, decay_ref, beta_ref
    )
    beta_row, enter_row, key_row = rows_of
    cum_col, beta_col, key_col, enters, leaves = columns_of
    square = (TOK, TOK)
    heads = range(HEADS_STEP)
    strict = rows > cols
    eye = (rows == cols).astype(F32)
    inner = [x * r for x, r in zip(inner, key_row)]
    system = [
        jnp.where(strict, (beta_col[h] * key_col[h // 2]) * decay[h] * inner[h // 2], 0.0)
        for h in heads
    ]
    system_bf = [x.astype(BF16) for x in system]
    zero_bf = jnp.zeros(square, BF16)
    inverse = [eye.astype(BF16)] * HEADS_STEP
    size = 1
    while size < TOK:
        mask = (rows // (2 * size) == cols // (2 * size)) & (rows // size != cols // size)
        inside = [jnp.where(mask, x, zero_bf) for x in system_bf]
        if size > 1:
            inside = [dot_nn(x, y).astype(BF16) for x, y in zip(inside, inverse)]
            inside = [dot_nn(y, x).astype(BF16) for x, y in zip(inside, inverse)]
        inverse = [y - x for x, y in zip(inside, inverse)]
        size *= 2
    residual = [
        (eye - inverse[h].astype(F32) - dot_nn(wide(system[h]), twice(inverse[h], 0))).astype(BF16)
        for h in heads
    ]
    solve = [inverse[h].astype(F32) + dot_nn(inverse[h], residual[h]) for h in heads]
    for h in heads:
        solve_ref[h] = solve[h]

    key_pair = [twice(k, 0) for k in key]
    key_t_pair = [twice(k.T, 1) for k in key]
    value_t = [v_ref[:, h * DV : (h + 1) * DV].T for h in heads]
    weight_row = [beta_row[h : h + 1] * enter_row[h : h + 1] * key_row[h // 2] for h in heads]
    leave_col = [
        jnp.where(leaves, jnp.exp(jnp.minimum(cum_col[h][TOK - 1 :] - cum_col[h], 0.0)), 0.0)
        * key_col[h // 2]
        for h in heads
    ]
    left = [leave_col[h] * solve[h] for h in heads]
    offset_in = [dot_nt(twice(value_t[h], 1), wide(left[h] * beta_row[h : h + 1])) for h in heads]
    change_in = [dot_nt(key_t_pair[h // 2], wide(left[h] * weight_row[h])) for h in heads]
    offset = [dot_nn(wide(offset_in[h]), key_pair[h // 2]).astype(BF16) for h in heads]
    change = [dot_nn(wide(change_in[h]), key_pair[h // 2]).astype(BF16) for h in heads]
    at_row = iota((16, TOK), 0)
    for h in heads:
        keep = jnp.broadcast_to(enter_row[h : h + 1, TOK - 1 :], (16, TOK))
        keep_high = keep.astype(BF16)
        keep_mid, keep_low = halves(keep - keep_high.astype(F32))
        terms = jnp.where(
            at_row == 0,
            keep_high.astype(F32),
            jnp.where(
                at_row == 1,
                keep_mid.astype(F32),
                jnp.where(at_row == 2, keep_low.astype(F32), 0.0),
            ),
        ).astype(BF16)
        for s in range(2):
            maps_ref[2 * h + s, 0:64, :] = offset[h][s * 64 : (s + 1) * 64]
            maps_ref[2 * h + s, 64:192, :] = change[h]
            maps_ref[2 * h + s, 192:208, :] = terms


def reads_kernel(
    len_ref, q_ref, k_ref, v_ref, decay_ref, beta_ref, solve_ref, query_ref, local_ref
):
    rows, cols, key, inner, decay, rows_of, columns_of = block_frame(
        len_ref, k_ref, decay_ref, beta_ref
    )
    beta_row, enter_row, key_row = rows_of
    cum_col, beta_col, key_col, enters, leaves = columns_of
    heads = range(HEADS_STEP)
    query = [q_ref[:, i * DK : (i + 1) * DK] for i in range(HEADS_STEP // 2)]
    query_f = [q.astype(F32) for q in query]
    query_col = [
        lax.rsqrt(jnp.sum(q * q, 1, keepdims=True) + EPSILON) * (DK**-0.5) for q in query_f
    ]
    cross = [dot_nt(q, k) * r * c for q, k, r, c in zip(query, key, key_row, query_col)]
    key_pair = [twice(k, 0) for k in key]
    value = [v_ref[:, h * DV : (h + 1) * DV] for h in heads]
    weight_row = [beta_row[h : h + 1] * enter_row[h : h + 1] * key_row[h // 2] for h in heads]
    mixed = []
    for h in heads:
        score_high, score_low = halves(decay[h] * cross[h // 2])
        solve_high, solve_low = halves(solve_ref[h])
        mixed.append(
            dot_nn(
                jnp.concatenate([score_high, score_low, score_high], axis=1),
                jnp.concatenate([solve_high, solve_high, solve_low], axis=0),
            )
        )
    for h in heads:
        local_ref[:, h * DV : (h + 1) * DV] = dot_nn(
            wide(mixed[h] * beta_row[h : h + 1]), twice(value[h], 0)
        )
    for h in heads:
        enter_col = jnp.where(enters, jnp.exp(cum_col[h]), 0.0) * query_col[h // 2]
        query_ref[h] = enter_col * query_f[h // 2] - dot_nn(
            wide(mixed[h] * weight_row[h]), key_pair[h // 2]
        )


STEPS = HV // HEADS_STEP
LENGTHS = pl.BlockSpec(memory_space=pltpu.SMEM)
KEY_BLOCK = pl.BlockSpec((TOK, HK * DK // STEPS), lambda i: (0, i))
VALUE_BLOCK = pl.BlockSpec((TOK, HV * DV // STEPS), lambda i: (0, i))
HEAD_BLOCK = pl.BlockSpec((HEADS_STEP, TOK), lambda i: (i, 0))
SQUARE_BLOCK = pl.BlockSpec((HEADS_STEP, TOK, TOK), lambda i: (i, 0, 0))


def maps_call(lengths, key_in, value_in, log_decay, beta_logit):
    return pl.pallas_call(
        maps_kernel,
        grid=(STEPS,),
        in_specs=[LENGTHS, KEY_BLOCK, VALUE_BLOCK, HEAD_BLOCK, HEAD_BLOCK],
        out_specs=[
            pl.BlockSpec((2 * HEADS_STEP, MAP_ROWS, DK), lambda i: (i, 0, 0)),
            SQUARE_BLOCK,
        ],
        out_shape=[
            jax.ShapeDtypeStruct((2 * HV, MAP_ROWS, DK), BF16),
            jax.ShapeDtypeStruct((HV, TOK, TOK), F32),
        ],
        compiler_params=params(),
        name="block_maps",
    )(lengths, key_in, value_in, log_decay, beta_logit)


def reads_call(lengths, queries, key_in, value_in, log_decay, beta_logit, solve):
    return pl.pallas_call(
        reads_kernel,
        grid=(STEPS,),
        in_specs=[
            LENGTHS,
            KEY_BLOCK,
            KEY_BLOCK,
            VALUE_BLOCK,
            HEAD_BLOCK,
            HEAD_BLOCK,
            SQUARE_BLOCK,
        ],
        out_specs=[SQUARE_BLOCK, VALUE_BLOCK],
        out_shape=[
            jax.ShapeDtypeStruct((HV, TOK, DK), F32),
            jax.ShapeDtypeStruct((TOK, HV * DV), F32),
        ],
        compiler_params=params(),
        name="block_reads",
    )(lengths, queries, key_in, value_in, log_decay, beta_logit, solve)


def scan_kernel(maps_ref, out_ref):
    blocks = maps_ref.shape[0]
    state = jnp.zeros((64, DK), F32)
    for at in range(blocks):
        high, low = halves(state)
        out_ref[at * 64 : (at + 1) * 64, :] = high
        if at < blocks - 1:
            offset = maps_ref[at, 0:64, :].astype(F32)
            change = maps_ref[at, 64:192, :]
            keep = jnp.sum(maps_ref[at, 192:208, :].astype(F32), 0, keepdims=True)
            moved = dot_nn(jnp.concatenate([high, low], axis=0), change)
            state = keep * state - (moved[:64] + moved[64:]) + offset


def scan_call(maps):
    blocks = maps.shape[0]
    return pl.pallas_call(
        scan_kernel,
        out_shape=jax.ShapeDtypeStruct((blocks * 64, DK), BF16),
        compiler_params=params(),
        name="state_scan",
    )(maps)


def finish_kernel(
    gain_ref,
    post_ref,
    code_ref,
    state_hbm,
    query_hbm,
    local_hbm,
    gate_hbm,
    resid_hbm,
    proj_hbm,
    hidden_hbm,
    out_hbm,
    state_ref,
    query_ref,
    local_ref,
    gate_ref,
    resid_ref,
    weight_ref,
    hidden_ref,
    rows_ref,
    out_ref,
    sems,
    weight_sems,
    hidden_sem,
    out_sems,
):
    loads = [
        pltpu.make_async_copy(source, target, sems.at[i])
        for i, (source, target) in enumerate(
            [
                (state_hbm, state_ref),
                (query_hbm, query_ref),
                (local_hbm, local_ref),
                (gate_hbm, gate_ref),
                (resid_hbm, resid_ref),
            ]
        )
    ]
    quarters = []
    for g in range(GROUPS):
        at = (slice(None), pl.ds(g * WIDTH, WIDTH))
        quarters.append(
            pltpu.make_async_copy(proj_hbm.at[at], weight_ref.at[at], weight_sems.at[g])
        )
    for load in loads:
        load.start()
    quarters[0].start()
    for load in loads:
        load.wait()
    quarters[1].start()
    gain = gain_ref[...]
    normed = []
    for h in range(HV):
        cut = slice(h * DV, (h + 1) * DV)
        outputs = local_ref[:, cut] + dot_nt(wide(query_ref[h]), twice(state_ref[cut, :], 1))
        scale = lax.rsqrt(jnp.mean(outputs * outputs, -1, keepdims=True) + EPSILON)
        gate = gate_ref[:, cut].astype(F32)
        normed.append((outputs * scale * gain * (gate / (1.0 + jnp.exp(-gate)))).astype(BF16))
    normed = jnp.concatenate(normed, axis=1)
    total = jnp.zeros((TOK, 1), F32)
    parts = []
    for g in range(GROUPS):
        cut = slice(g * WIDTH, (g + 1) * WIDTH)
        quarters[g].wait()
        if g + 2 < GROUPS:
            quarters[g + 2].start()
        mixed = dot_nn(normed, weight_ref[:, cut])
        hidden = (resid_ref[:, cut].astype(F32) + mixed).astype(BF16)
        hidden_ref[:, cut] = hidden
        hidden = hidden.astype(F32)
        total = total + jnp.sum(hidden * hidden, -1, keepdims=True)
        parts.append(hidden)
    keep = pltpu.make_async_copy(hidden_ref, hidden_hbm, hidden_sem)
    keep.start()
    scale = lax.rsqrt(total / D + EPSILON)
    for g in range(GROUPS):
        cut = slice(g * WIDTH, (g + 1) * WIDTH)
        rows_ref[g * TOK : (g + 1) * TOK, :] = (parts[g] * scale * post_ref[:, cut]).astype(BF16)

    count = code_ref.shape[0] // DISPATCH_STEPS
    stores = [keep]
    for step in range(DISPATCH_STEPS):
        code = code_ref[step * count : (step + 1) * count, :][:, None, :]
        tiles = []
        for part in range(SPAN // 8):
            at = iota((1, 8, TOK), 1) + 8 * part
            slot, group = at % CAP, at // CAP
            pick = [
                jnp.where(code == jnp.where(group == g, slot, TOK).astype(F32), 1.0, 0.0)
                .reshape(count * 8, TOK)
                .astype(BF16)
                for g in (part, part + 1)
            ]
            source = rows_ref[part * TOK : (part + 2) * TOK, :]
            tiles.append(dot_nn(jnp.concatenate(pick, axis=1), source).reshape(count, 1, 8, WIDTH))
        at = pl.ds(step * count * SPAN, count * SPAN)
        out_ref[at, :] = jnp.concatenate(tiles, axis=1).reshape(count * SPAN, WIDTH).astype(BF16)
        stores.append(pltpu.make_async_copy(out_ref.at[at], out_hbm.at[at], out_sems.at[step]))
        stores[-1].start()
    for store in stores:
        store.wait()


def finish_call(state, query, local, gate_in, residual_in, head_gain, post_gain, code_t, out_proj):
    experts = code_t.shape[0]
    large = [state, query, local, gate_in, residual_in]
    hidden = jax.ShapeDtypeStruct((TOK, D), BF16)
    sent = jax.ShapeDtypeStruct((experts * SPAN, WIDTH), BF16)
    rows = jax.ShapeDtypeStruct((GROUPS * TOK, WIDTH), BF16)
    return pl.pallas_call(
        finish_kernel,
        in_specs=[pl.BlockSpec(memory_space=pltpu.VMEM)] * 3
        + [pl.BlockSpec(memory_space=pl.ANY)] * 6,
        out_specs=[pl.BlockSpec(memory_space=pl.ANY)] * 2,
        out_shape=[hidden, sent],
        scratch_shapes=[
            pltpu.VMEM(x.shape, x.dtype) for x in large + [out_proj, hidden, rows, sent]
        ]
        + [
            pltpu.SemaphoreType.DMA((len(large),)),
            pltpu.SemaphoreType.DMA((GROUPS,)),
            pltpu.SemaphoreType.DMA,
            pltpu.SemaphoreType.DMA((DISPATCH_STEPS,)),
        ],
        compiler_params=params(),
        name="mixer_finish",
    )(head_gain, post_gain, code_t, *large, out_proj)


def route_kernel(routes_ref, gates_ref, code_ref, code_t_ref):
    experts = code_t_ref.shape[0]
    expert = iota((TOK, experts), 1)
    hit = jnp.zeros((TOK, experts), F32)
    gate = jnp.zeros((TOK, experts), F32)
    for k in range(TOPK):
        match = routes_ref[:, k : k + 1] == expert
        hit = jnp.where(match, 1.0, hit)
        gate = jnp.where(match, gates_ref[:, k : k + 1], gate)
    square = (TOK, TOK)
    before = (iota(square, 0) > iota(square, 1)).astype(BF16)
    rank = dot_nn(before, hit.astype(BF16))
    code = jnp.where(hit > 0.0, rank, -1.0)
    code_ref[0:TOK, :] = code.astype(BF16)
    code_ref[TOK:, :] = gate.astype(BF16)
    for at in range(0, experts, TOK):
        code_t_ref[at : at + TOK, :] = code[:, at : at + TOK].T


def route_call(routes, gates, experts):
    return pl.pallas_call(
        route_kernel,
        out_shape=[
            jax.ShapeDtypeStruct((2 * TOK, experts), BF16),
            jax.ShapeDtypeStruct((experts, TOK), F32),
        ],
        compiler_params=params(),
        name="routing",
    )(routes, gates)


def expert_kernel(
    rows_hbm,
    in_hbm,
    out_hbm,
    result_hbm,
    rows_ref,
    result_ref,
    x_ref,
    y_ref,
    in_vmem,
    out_vmem,
    row_sem,
    in_sem,
    out_sem,
    result_sem,
):
    local = in_vmem.shape[0]
    total = rows_ref.shape[0]
    half = total // 2
    halves_in = []
    for part in range(2):
        at = pl.ds(part * half, half)
        halves_in.append(
            pltpu.make_async_copy(rows_hbm.at[at], rows_ref.at[at], row_sem.at[part])
        )
    loads = []
    for j in range(local):
        loads.append(
            (
                pltpu.make_async_copy(in_hbm.at[j], in_vmem.at[j], in_sem.at[j]),
                pltpu.make_async_copy(out_hbm.at[j], out_vmem.at[j], out_sem.at[j]),
            )
        )
    halves_in[0].start()
    for first, second in loads:
        first.start()
        second.start()
    halves_in[1].start()

    block_rows = local * GROUP_ROWS
    count = half // block_rows
    square = (block_rows, block_rows)
    to_at, from_at = iota(square, 0), iota(square, 1)

    def source_of(at):
        piece, rest = at // PIECE, at % PIECE
        return (rest // CAP) * (local * SPAN) + piece * CAP + rest % CAP

    order = (source_of(to_at) == from_at).astype(BF16)
    back = (source_of(from_at) == to_at).astype(BF16)
    stores = []
    for part in range(2):
        base = part * half
        halves_in[part].wait()
        for i in range(0, count, 2):
            moved = [
                dot_nn(order, rows_ref[base + k * block_rows : base + (k + 1) * block_rows, :])
                for k in (i, i + 1)
            ]
            for j in range(local):
                for g in range(GROUPS):
                    cut = slice((j * GROUPS + g) * PIECE, (j * GROUPS + g + 1) * PIECE)
                    x_ref[j, i * PIECE : (i + 2) * PIECE, g * WIDTH : (g + 1) * WIDTH] = (
                        jnp.concatenate([m[cut] for m in moved], axis=0).astype(BF16)
                    )
        for j in range(local):
            x = x_ref[j]
            if part == 0:
                loads[j][0].wait()
            gate = dot_nn(x, in_vmem[j, :, :FF])
            up = dot_nn(x, in_vmem[j, :, FF:])
            hidden = (gate / (1.0 + jnp.exp(-gate)) * up).astype(BF16)
            if part == 0:
                loads[j][1].wait()
            y_ref[j] = dot_nn(hidden, out_vmem[j])
        for i in range(count):
            block = jnp.concatenate(
                [
                    y_ref[j, i * PIECE : (i + 1) * PIECE, g * WIDTH : (g + 1) * WIDTH]
                    for j in range(local)
                    for g in range(GROUPS)
                ],
                axis=0,
            ).astype(BF16)
            at = pl.ds(base + i * block_rows, block_rows)
            result_ref[at, :] = dot_nn(back, block).astype(BF16)
            if i % 4 == 3:
                number = len(stores)
                at = pl.ds(base + (i - 3) * block_rows, 4 * block_rows)
                stores.append(
                    pltpu.make_async_copy(
                        result_ref.at[at], result_hbm.at[at], result_sem.at[number]
                    )
                )
                stores[-1].start()
    for store in stores:
        store.wait()


def expert_call(rows, expert_in, expert_out):
    total = rows.shape[0]
    local = expert_in.shape[0]
    tokens = total // (2 * GROUPS * local)
    stores = total // (4 * local * GROUP_ROWS)
    return pl.pallas_call(
        expert_kernel,
        in_specs=[pl.BlockSpec(memory_space=pl.ANY)] * 3,
        out_specs=pl.BlockSpec(memory_space=pl.ANY),
        out_shape=jax.ShapeDtypeStruct((total, WIDTH), BF16),
        scratch_shapes=[
            pltpu.VMEM((total, WIDTH), BF16),
            pltpu.VMEM((total, WIDTH), BF16),
            pltpu.VMEM((local, tokens, D), BF16),
            pltpu.VMEM((local, tokens, D), F32),
            pltpu.VMEM((local, D, 2 * FF), BF16),
            pltpu.VMEM((local, FF, D), BF16),
            pltpu.SemaphoreType.DMA((2,)),
            pltpu.SemaphoreType.DMA((local,)),
            pltpu.SemaphoreType.DMA((local,)),
            pltpu.SemaphoreType.DMA((stores,)),
        ],
        compiler_params=params(),
        name="experts",
    )(rows, expert_in, expert_out)


def combine_kernel(code_ref, rows_ref, hidden_ref, out_ref, total_ref):
    step = pl.program_id(0)
    tile = rows_ref.shape[0]
    experts = code_ref.shape[1]
    at = iota((1, tile), 1)
    spread = (at // SPAN + step * (tile // SPAN) == iota((experts, tile), 0)).astype(BF16)
    both = dot_nn(code_ref[...], spread)
    code, gate = both[:TOK], both[TOK:].astype(BF16)
    slot, group = at % CAP, at // CAP % GROUPS
    zero = jnp.zeros((TOK, tile), BF16)
    weights = [
        jnp.where(code == jnp.where(group == g, slot, TOK).astype(F32), gate, zero)
        for g in range(GROUPS)
    ]
    part = dot_nn(jnp.concatenate(weights, axis=0), rows_ref[...])

    @pl.when(step == 0)
    def _():
        total_ref[...] = part

    @pl.when(step > 0)
    def _():
        total_ref[...] += part

    @pl.when(step == pl.num_programs(0) - 1)
    def _():
        for g in range(GROUPS):
            cut = slice(g * WIDTH, (g + 1) * WIDTH)
            mix = total_ref[g * TOK : (g + 1) * TOK, :]
            out_ref[:, cut] = (hidden_ref[:, cut].astype(F32) + mix).astype(BF16)


def combine_call(code, rows, hidden):
    total = rows.shape[0]
    steps = 4
    return pl.pallas_call(
        combine_kernel,
        grid=(steps,),
        in_specs=[
            pl.BlockSpec(code.shape, lambda i: (0, 0)),
            pl.BlockSpec((total // steps, WIDTH), lambda i: (i, 0)),
            pl.BlockSpec((TOK, D), lambda i: (0, 0)),
        ],
        out_specs=pl.BlockSpec((TOK, D), lambda i: (0, 0)),
        out_shape=jax.ShapeDtypeStruct((TOK, D), BF16),
        scratch_shapes=[pltpu.VMEM((GROUPS * TOK, WIDTH), F32)],
        compiler_params=params(),
        name="combine",
    )(code, rows, hidden)


def exchange(rows, axes):
    return lax.all_to_all(rows, axes, split_axis=0, concat_axis=0, tiled=True)


def per_device(
    queries,
    key_in,
    value_in,
    gate_in,
    residual_in,
    log_decay,
    beta_logit,
    lengths,
    head_gain,
    out_proj,
    post_gain,
    expert_in,
    expert_out,
    routes,
    route_gates,
):
    devices = lax.axis_size("dp") * lax.axis_size("ctx")
    local = expert_in.shape[0]
    shared = (key_in[0], value_in[0], log_decay[0], beta_logit[0])
    maps, solve = maps_call(lengths, *shared)
    query, inside = reads_call(lengths, queries[0], *shared, solve)
    code, code_t = route_call(routes[0], route_gates[0], local * devices)
    states = exchange(scan_call(exchange(maps, "ctx")), "ctx")
    hidden, sent = finish_call(
        states,
        query,
        inside,
        gate_in[0],
        residual_in[0],
        head_gain[None],
        post_gain[None],
        code_t,
        out_proj,
    )
    both = ("dp", "ctx")
    arrived = exchange(sent.reshape(devices, local * SPAN, WIDTH), both)
    results = expert_call(arrived.reshape(sent.shape), expert_in, expert_out)
    returned = exchange(results.reshape(devices, local * SPAN, WIDTH), both)
    return combine_call(code, returned.reshape(sent.shape), hidden)[None]


def solution(mesh):
    tokens = P("dp", "ctx", None)
    heads = P("dp", None, "ctx")
    experts = P(("dp", "ctx"), None, None)
    in_specs = (tokens,) * 5 + (heads, heads, P("dp", None), P(), P(), P())
    in_specs += (experts, experts, tokens, tokens)
    return jax.shard_map(
        per_device, mesh=mesh, in_specs=in_specs, out_specs=tokens, check_vma=False
    )
```

```python
import jax
import jax.numpy as jnp
from jax import lax
from jax.experimental import pallas as pl
from jax.experimental.pallas import tpu as pltpu
from jax.sharding import PartitionSpec as P

D = 2048
DK = 128
DV = 128
FF = 512
TOPK = 10
HK = 8
HV = 16
TOK = 128
CAP = 6
GROUPS = 4
WIDTH = D // GROUPS
SPAN = GROUPS * CAP
EPSILON = 1e-06

F32 = jnp.float32
BF16 = jnp.bfloat16
HEADS_STEP = 16
MAP_ROWS = DV + DK + 16
SRC_GROUP = 4
GROUP_ROWS = SRC_GROUP * SPAN
PIECE = SRC_GROUP * CAP
DISPATCH_STEPS = 8
COMBINE_PARTS = 2
MIB = 1 << 20


def dot_nn(a, b):
    return lax.dot_general(a, b, (((1,), (0,)), ((), ())), preferred_element_type=F32)


def dot_nt(a, b):
    return lax.dot_general(a, b, (((1,), (1,)), ((), ())), preferred_element_type=F32)


def halves(x):
    high = x.astype(BF16)
    return high, (x - high.astype(F32)).astype(BF16)


def wide(x):
    high, low = halves(x)
    return jnp.concatenate([high, low], axis=1)


def twice(x, axis):
    return jnp.concatenate([x, x], axis=axis)


def iota(shape, axis):
    return lax.broadcasted_iota(jnp.int32, shape, axis)


def params(limit=60 * MIB):
    return pltpu.CompilerParams(vmem_limit_bytes=limit)


def block_frame(len_ref, k_ref, decay_ref, beta_ref):
    first = lax.axis_index("ctx") * TOK
    start1 = len_ref[0, 0]
    start2 = start1 + len_ref[0, 1]
    start3 = start2 + len_ref[0, 2]

    def segment(at):
        return (
            (at >= 0).astype(jnp.int32)
            + (at >= start1).astype(jnp.int32)
            + (at >= start2).astype(jnp.int32)
            + (at >= start3).astype(jnp.int32)
        )

    square = (TOK, TOK)
    rows, cols = iota(square, 0), iota(square, 1)
    seg_before, seg_last = segment(first - 1), segment(first + TOK - 1)
    lower = (segment(first + rows) == segment(first + cols)) & (rows >= cols)
    cum_row = lax.dot_general(
        decay_ref[...],
        (rows <= cols).astype(F32),
        (((1,), (0,)), ((), ())),
        precision=lax.Precision.HIGHEST,
        preferred_element_type=F32,
    )
    beta_row = 1.0 / (1.0 + jnp.exp(-beta_ref[...]))
    columns = jnp.concatenate(
        [cum_row, beta_row, jnp.zeros((TOK - 2 * HEADS_STEP, TOK), F32)], axis=0
    ).T
    row8 = iota((HEADS_STEP, TOK), 1)
    enter_row = jnp.where(segment(first + row8) == seg_before, jnp.exp(cum_row), 0.0)
    at = first + iota((TOK, 1), 0)
    enters, leaves = segment(at) == seg_before, segment(at) == seg_last
    cum_col = [columns[:, h : h + 1] for h in range(HEADS_STEP)]
    beta_col = [columns[:, HEADS_STEP + h : HEADS_STEP + h + 1] for h in range(HEADS_STEP)]
    key = [k_ref[:, i * DK : (i + 1) * DK] for i in range(HEADS_STEP // 2)]
    inner = [dot_nt(k, k) for k in key]
    squares = [jnp.where(rows == cols, x, 0.0) for x in inner]
    key_row = [lax.rsqrt(jnp.sum(x, 0, keepdims=True) + EPSILON) for x in squares]
    key_col = [lax.rsqrt(jnp.sum(x, 1, keepdims=True) + EPSILON) for x in squares]
    decay = [
        jnp.where(
            lower, jnp.exp(jnp.minimum(cum_col[h] - cum_row[h : h + 1], 0.0)), 0.0
        )
        for h in range(HEADS_STEP)
    ]
    rows_of = (beta_row, enter_row, key_row)
    columns_of = (cum_col, beta_col, key_col, enters, leaves)
    return rows, cols, key, inner, decay, rows_of, columns_of


def maps_kernel(len_ref, k_ref, v_ref, decay_ref, beta_ref, maps_ref, solve_ref):
    rows, cols, key, inner, decay, rows_of, columns_of = block_frame(
        len_ref, k_ref, decay_ref, beta_ref
    )
    beta_row, enter_row, key_row = rows_of
    cum_col, beta_col, key_col, enters, leaves = columns_of
    square = (TOK, TOK)
    heads = range(HEADS_STEP)
    strict = rows > cols
    eye = (rows == cols).astype(F32)
    inner = [x * r for x, r in zip(inner, key_row)]
    system = [
        jnp.where(strict, (beta_col[h] * key_col[h // 2]) * decay[h] * inner[h // 2], 0.0)
        for h in heads
    ]
    system_bf = [x.astype(BF16) for x in system]
    zero_bf = jnp.zeros(square, BF16)
    inverse = [eye.astype(BF16)] * HEADS_STEP
    size = 1
    while size < TOK:
        mask = (rows // (2 * size) == cols // (2 * size)) & (rows // size != cols // size)
        inside = [jnp.where(mask, x, zero_bf) for x in system_bf]
        if size > 1:
            inside = [dot_nn(x, y).astype(BF16) for x, y in zip(inside, inverse)]
            inside = [dot_nn(y, x).astype(BF16) for x, y in zip(inside, inverse)]
        inverse = [y - x for x, y in zip(inside, inverse)]
        size *= 2
    residual = [
        (eye - inverse[h].astype(F32) - dot_nn(wide(system[h]), twice(inverse[h], 0))).astype(BF16)
        for h in heads
    ]
    solve = [inverse[h].astype(F32) + dot_nn(inverse[h], residual[h]) for h in heads]
    for h in heads:
        solve_ref[h] = solve[h]

    key_pair = [twice(k, 0) for k in key]
    key_t_pair = [twice(k.T, 1) for k in key]
    value_t = [v_ref[:, h * DV : (h + 1) * DV].T for h in heads]
    weight_row = [beta_row[h : h + 1] * enter_row[h : h + 1] * key_row[h // 2] for h in heads]
    leave_col = [
        jnp.where(leaves, jnp.exp(jnp.minimum(cum_col[h][TOK - 1 :] - cum_col[h], 0.0)), 0.0)
        * key_col[h // 2]
        for h in heads
    ]
    left = [leave_col[h] * solve[h] for h in heads]
    offset_in = [dot_nt(twice(value_t[h], 1), wide(left[h] * beta_row[h : h + 1])) for h in heads]
    change_in = [dot_nt(key_t_pair[h // 2], wide(left[h] * weight_row[h])) for h in heads]
    offset = [dot_nn(wide(offset_in[h]), key_pair[h // 2]).astype(BF16) for h in heads]
    change = [dot_nn(wide(change_in[h]), key_pair[h // 2]).astype(BF16) for h in heads]
    at_row = iota((16, TOK), 0)
    for h in heads:
        keep = jnp.broadcast_to(enter_row[h : h + 1, TOK - 1 :], (16, TOK))
        keep_high = keep.astype(BF16)
        keep_mid, keep_low = halves(keep - keep_high.astype(F32))
        terms = jnp.where(
            at_row == 0,
            keep_high.astype(F32),
            jnp.where(
                at_row == 1,
                keep_mid.astype(F32),
                jnp.where(at_row == 2, keep_low.astype(F32), 0.0),
            ),
        ).astype(BF16)
        maps_ref[h, 0:DV, :] = offset[h]
        maps_ref[h, DV : DV + DK, :] = change[h]
        maps_ref[h, DV + DK :, :] = terms


def reads_kernel(
    len_ref, q_ref, k_ref, v_ref, decay_ref, beta_ref, solve_ref, query_ref, local_ref
):
    rows, cols, key, inner, decay, rows_of, columns_of = block_frame(
        len_ref, k_ref, decay_ref, beta_ref
    )
    beta_row, enter_row, key_row = rows_of
    cum_col, beta_col, key_col, enters, leaves = columns_of
    heads = range(HEADS_STEP)
    query = [q_ref[:, i * DK : (i + 1) * DK] for i in range(HEADS_STEP // 2)]
    query_f = [q.astype(F32) for q in query]
    query_col = [
        lax.rsqrt(jnp.sum(q * q, 1, keepdims=True) + EPSILON) * (DK**-0.5) for q in query_f
    ]
    cross = [dot_nt(q, k) * r * c for q, k, r, c in zip(query, key, key_row, query_col)]
    key_pair = [twice(k, 0) for k in key]
    value = [v_ref[:, h * DV : (h + 1) * DV] for h in heads]
    weight_row = [beta_row[h : h + 1] * enter_row[h : h + 1] * key_row[h // 2] for h in heads]
    mixed = []
    for h in heads:
        score_high, score_low = halves(decay[h] * cross[h // 2])
        solve_high, solve_low = halves(solve_ref[h])
        mixed.append(
            dot_nn(
                jnp.concatenate([score_high, score_low, score_high], axis=1),
                jnp.concatenate([solve_high, solve_high, solve_low], axis=0),
            )
        )
    for h in heads:
        local_ref[:, h * DV : (h + 1) * DV] = dot_nn(
            wide(mixed[h] * beta_row[h : h + 1]), twice(value[h], 0)
        ).astype(BF16)
    for h in heads:
        enter_col = jnp.where(enters, jnp.exp(cum_col[h]), 0.0) * query_col[h // 2]
        read = dot_nn(wide(mixed[h] * weight_row[h]), key_pair[h // 2])
        query_ref[h] = (enter_col * query_f[h // 2] - read).astype(BF16)


STEPS = HV // HEADS_STEP
LENGTHS = pl.BlockSpec(memory_space=pltpu.SMEM)
KEY_BLOCK = pl.BlockSpec((TOK, HK * DK // STEPS), lambda i: (0, i))
VALUE_BLOCK = pl.BlockSpec((TOK, HV * DV // STEPS), lambda i: (0, i))
HEAD_BLOCK = pl.BlockSpec((HEADS_STEP, TOK), lambda i: (i, 0))
SQUARE_BLOCK = pl.BlockSpec((HEADS_STEP, TOK, TOK), lambda i: (i, 0, 0))


def maps_call(lengths, key_in, value_in, log_decay, beta_logit):
    return pl.pallas_call(
        maps_kernel,
        grid=(STEPS,),
        in_specs=[LENGTHS, KEY_BLOCK, VALUE_BLOCK, HEAD_BLOCK, HEAD_BLOCK],
        out_specs=[
            pl.BlockSpec((HEADS_STEP, MAP_ROWS, DK), lambda i: (i, 0, 0)),
            SQUARE_BLOCK,
        ],
        out_shape=[
            jax.ShapeDtypeStruct((HV, MAP_ROWS, DK), BF16),
            jax.ShapeDtypeStruct((HV, TOK, TOK), F32),
        ],
        compiler_params=params(),
        name="block_maps",
    )(lengths, key_in, value_in, log_decay, beta_logit)


def reads_call(lengths, queries, key_in, value_in, log_decay, beta_logit, solve):
    return pl.pallas_call(
        reads_kernel,
        grid=(STEPS,),
        in_specs=[
            LENGTHS,
            KEY_BLOCK,
            KEY_BLOCK,
            VALUE_BLOCK,
            HEAD_BLOCK,
            HEAD_BLOCK,
            SQUARE_BLOCK,
        ],
        out_specs=[SQUARE_BLOCK, VALUE_BLOCK],
        out_shape=[
            jax.ShapeDtypeStruct((HV, TOK, DK), BF16),
            jax.ShapeDtypeStruct((TOK, HV * DV), BF16),
        ],
        compiler_params=params(),
        name="block_reads",
    )(lengths, queries, key_in, value_in, log_decay, beta_logit, solve)


def scan_kernel(own_ref, other_ref, out_ref):
    chips = own_ref.shape[0]
    even = lax.axis_index("ctx") % 2 == 0
    state = jnp.zeros((DV, DK), F32)
    for chip in range(chips):
        own, other = own_ref[chip], other_ref[chip]
        entering = []
        for block in (jnp.where(even, own, other), jnp.where(even, other, own)):
            high, low = halves(state)
            entering.append(high)
            keep = jnp.sum(block[DV + DK :].astype(F32), 0, keepdims=True)
            moved = dot_nn(jnp.concatenate([high, low], axis=0), block[DV : DV + DK])
            state = keep * state + block[:DV].astype(F32) - (moved[:DV] + moved[DV:])
        out_ref[chip * DV : (chip + 1) * DV, :] = jnp.where(even, entering[0], entering[1])


def scan_call(own, other):
    return pl.pallas_call(
        scan_kernel,
        out_shape=jax.ShapeDtypeStruct((own.shape[0] * DV, DK), BF16),
        compiler_params=params(24 * MIB),
        name="state_scan",
    )(own, other)


def finish_kernel(
    gain_ref,
    post_ref,
    code_ref,
    state_hbm,
    query_hbm,
    local_hbm,
    gate_hbm,
    resid_hbm,
    proj_hbm,
    hidden_hbm,
    out_hbm,
    state_ref,
    query_ref,
    local_ref,
    gate_ref,
    resid_ref,
    weight_ref,
    hidden_ref,
    rows_ref,
    out_ref,
    sems,
    weight_sems,
    hidden_sem,
    out_sems,
):
    loads = [
        pltpu.make_async_copy(source, target, sems.at[i])
        for i, (source, target) in enumerate(
            [
                (state_hbm, state_ref),
                (query_hbm, query_ref),
                (local_hbm, local_ref),
                (gate_hbm, gate_ref),
                (resid_hbm, resid_ref),
            ]
        )
    ]
    quarters = []
    for g in range(GROUPS):
        at = (slice(None), pl.ds(g * WIDTH, WIDTH))
        quarters.append(
            pltpu.make_async_copy(proj_hbm.at[at], weight_ref.at[at], weight_sems.at[g])
        )
    for load in loads:
        load.start()
    quarters[0].start()
    for load in loads:
        load.wait()
    quarters[1].start()
    gain = gain_ref[...]
    normed = []
    for h in range(HV):
        cut = slice(h * DV, (h + 1) * DV)
        outputs = local_ref[:, cut].astype(F32) + dot_nt(query_ref[h], state_ref[cut, :])
        scale = lax.rsqrt(jnp.mean(outputs * outputs, -1, keepdims=True) + EPSILON)
        gate = gate_ref[:, cut].astype(F32)
        normed.append((outputs * scale * gain * (gate / (1.0 + jnp.exp(-gate)))).astype(BF16))
    normed = jnp.concatenate(normed, axis=1)
    total = jnp.zeros((TOK, 1), F32)
    parts = []
    for g in range(GROUPS):
        cut = slice(g * WIDTH, (g + 1) * WIDTH)
        quarters[g].wait()
        if g + 2 < GROUPS:
            quarters[g + 2].start()
        mixed = dot_nn(normed, weight_ref[:, cut])
        hidden = (resid_ref[:, cut].astype(F32) + mixed).astype(BF16)
        hidden_ref[:, cut] = hidden
        hidden = hidden.astype(F32)
        total = total + jnp.sum(hidden * hidden, -1, keepdims=True)
        parts.append(hidden)
    keep = pltpu.make_async_copy(hidden_ref, hidden_hbm, hidden_sem)
    keep.start()
    scale = lax.rsqrt(total / D + EPSILON)
    for g in range(GROUPS):
        cut = slice(g * WIDTH, (g + 1) * WIDTH)
        rows_ref[g * TOK : (g + 1) * TOK, :] = (parts[g] * scale * post_ref[:, cut]).astype(BF16)

    count = code_ref.shape[0] // DISPATCH_STEPS
    stores = [keep]
    for step in range(DISPATCH_STEPS):
        code = code_ref[step * count : (step + 1) * count, :][:, None, :]
        tiles = []
        for part in range(SPAN // 8):
            at = iota((1, 8, TOK), 1) + 8 * part
            slot, group = at % CAP, at // CAP
            pick = [
                jnp.where(code == jnp.where(group == g, slot, TOK).astype(F32), 1.0, 0.0)
                .reshape(count * 8, TOK)
                .astype(BF16)
                for g in (part, part + 1)
            ]
            source = rows_ref[part * TOK : (part + 2) * TOK, :]
            tiles.append(dot_nn(jnp.concatenate(pick, axis=1), source).reshape(count, 1, 8, WIDTH))
        at = pl.ds(step * count * SPAN, count * SPAN)
        out_ref[at, :] = jnp.concatenate(tiles, axis=1).reshape(count * SPAN, WIDTH).astype(BF16)
        stores.append(pltpu.make_async_copy(out_ref.at[at], out_hbm.at[at], out_sems.at[step]))
        stores[-1].start()
    for store in stores:
        store.wait()


def finish_call(state, query, local, gate_in, residual_in, head_gain, post_gain, code_t, out_proj):
    experts = code_t.shape[0]
    large = [state, query, local, gate_in, residual_in]
    hidden = jax.ShapeDtypeStruct((TOK, D), BF16)
    sent = jax.ShapeDtypeStruct((experts * SPAN, WIDTH), BF16)
    rows = jax.ShapeDtypeStruct((GROUPS * TOK, WIDTH), BF16)
    return pl.pallas_call(
        finish_kernel,
        in_specs=[pl.BlockSpec(memory_space=pltpu.VMEM)] * 3
        + [pl.BlockSpec(memory_space=pl.ANY)] * 6,
        out_specs=[pl.BlockSpec(memory_space=pl.ANY)] * 2,
        out_shape=[hidden, sent],
        scratch_shapes=[
            pltpu.VMEM(x.shape, x.dtype) for x in large + [out_proj, hidden, rows, sent]
        ]
        + [
            pltpu.SemaphoreType.DMA((len(large),)),
            pltpu.SemaphoreType.DMA((GROUPS,)),
            pltpu.SemaphoreType.DMA,
            pltpu.SemaphoreType.DMA((DISPATCH_STEPS,)),
        ],
        compiler_params=params(),
        name="mixer_finish",
    )(head_gain, post_gain, code_t, *large, out_proj)


def route_kernel(routes_ref, gates_ref, code_ref, code_t_ref):
    experts = code_t_ref.shape[0]
    expert = iota((experts, TOK), 0)
    hit = jnp.zeros((experts, TOK), F32)
    gate = jnp.zeros((experts, TOK), F32)
    for k in range(TOPK):
        match = routes_ref[k : k + 1, :] == expert
        hit = jnp.where(match, 1.0, hit)
        gate = jnp.where(match, gates_ref[k : k + 1, :], gate)
    square = (TOK, TOK)
    before = (iota(square, 0) < iota(square, 1)).astype(BF16)
    rank = dot_nn(hit.astype(BF16), before)
    code = jnp.where(hit > 0.0, rank, -1.0)
    code_t_ref[...] = code
    for at in range(0, experts, TOK):
        cut = slice(at, at + TOK)
        code_ref[0:TOK, cut] = code[cut].T.astype(BF16)
        code_ref[TOK:, cut] = gate[cut].T.astype(BF16)


def route_call(routes, gates, experts):
    return pl.pallas_call(
        route_kernel,
        out_shape=[
            jax.ShapeDtypeStruct((2 * TOK, experts), BF16),
            jax.ShapeDtypeStruct((experts, TOK), F32),
        ],
        compiler_params=params(),
        name="routing",
    )(routes, gates)


def block_orders(local):
    block_rows = local * GROUP_ROWS
    square = (block_rows, block_rows)
    to_at, from_at = iota(square, 0), iota(square, 1)

    def source_of(at):
        piece, rest = at // PIECE, at % PIECE
        return (rest // CAP) * (local * SPAN) + piece * CAP + rest % CAP

    order = (source_of(to_at) == from_at).astype(BF16)
    back = (source_of(from_at) == to_at).astype(BF16)
    return order, back


def unpack_blocks(order, rows_ref, base, count, local, x_ref):
    block_rows = local * GROUP_ROWS
    for i in range(0, count, 2):
        moved = [
            dot_nn(order, rows_ref[base + k * block_rows : base + (k + 1) * block_rows, :])
            for k in (i, i + 1)
        ]
        for j in range(local):
            for g in range(GROUPS):
                cut = slice((j * GROUPS + g) * PIECE, (j * GROUPS + g + 1) * PIECE)
                x_ref[j, i * PIECE : (i + 2) * PIECE, g * WIDTH : (g + 1) * WIDTH] = (
                    jnp.concatenate([m[cut] for m in moved], axis=0).astype(BF16)
                )


def expert_kernel(
    rows_hbm,
    in_hbm,
    out_hbm,
    result_hbm,
    rows_ref,
    result_ref,
    x_ref,
    y_ref,
    in_vmem,
    out_vmem,
    row_sem,
    in_sem,
    out_sem,
    result_sem,
):
    local = in_vmem.shape[0]
    total = rows_ref.shape[0]
    half = total // 2
    halves_in = []
    for part in range(2):
        at = pl.ds(part * half, half)
        halves_in.append(
            pltpu.make_async_copy(rows_hbm.at[at], rows_ref.at[at], row_sem.at[part])
        )
    loads = []
    for j in range(local):
        loads.append(
            (
                pltpu.make_async_copy(in_hbm.at[j], in_vmem.at[j], in_sem.at[j]),
                pltpu.make_async_copy(out_hbm.at[j], out_vmem.at[j], out_sem.at[j]),
            )
        )
    halves_in[0].start()
    for first, second in loads:
        first.start()
        second.start()
    halves_in[1].start()

    block_rows = local * GROUP_ROWS
    count = half // block_rows
    order, back = block_orders(local)
    stores = []
    for part in range(2):
        base = part * half
        halves_in[part].wait()
        unpack_blocks(order, rows_ref, base, count, local, x_ref)
        for j in range(local):
            x = x_ref[j]
            if part == 0:
                loads[j][0].wait()
            gate = dot_nn(x, in_vmem[j, :, :FF])
            up = dot_nn(x, in_vmem[j, :, FF:])
            hidden = (gate / (1.0 + jnp.exp(-gate)) * up).astype(BF16)
            if part == 0:
                loads[j][1].wait()
            y_ref[j] = dot_nn(hidden, out_vmem[j])
        for i in range(count):
            block = jnp.concatenate(
                [
                    y_ref[j, i * PIECE : (i + 1) * PIECE, g * WIDTH : (g + 1) * WIDTH]
                    for j in range(local)
                    for g in range(GROUPS)
                ],
                axis=0,
            ).astype(BF16)
            at = pl.ds(base + i * block_rows, block_rows)
            result_ref[at, :] = dot_nn(back, block).astype(BF16)
            if i % 4 == 3:
                number = len(stores)
                at = pl.ds(base + (i - 3) * block_rows, 4 * block_rows)
                stores.append(
                    pltpu.make_async_copy(
                        result_ref.at[at], result_hbm.at[at], result_sem.at[number]
                    )
                )
                stores[-1].start()
    for store in stores:
        store.wait()


def expert_call(rows, expert_in, expert_out):
    total = rows.shape[0]
    local = expert_in.shape[0]
    tokens = total // (2 * GROUPS * local)
    stores = total // (4 * local * GROUP_ROWS)
    return pl.pallas_call(
        expert_kernel,
        in_specs=[pl.BlockSpec(memory_space=pl.ANY)] * 3,
        out_specs=pl.BlockSpec(memory_space=pl.ANY),
        out_shape=jax.ShapeDtypeStruct((total, WIDTH), BF16),
        scratch_shapes=[
            pltpu.VMEM((total, WIDTH), BF16),
            pltpu.VMEM((total, WIDTH), BF16),
            pltpu.VMEM((local, tokens, D), BF16),
            pltpu.VMEM((local, tokens, D), F32),
            pltpu.VMEM((local, D, 2 * FF), BF16),
            pltpu.VMEM((local, FF, D), BF16),
            pltpu.SemaphoreType.DMA((2,)),
            pltpu.SemaphoreType.DMA((local,)),
            pltpu.SemaphoreType.DMA((local,)),
            pltpu.SemaphoreType.DMA((stores,)),
        ],
        compiler_params=params(),
        name="experts",
    )(rows, expert_in, expert_out)


def combine_kernel(code_ref, hidden_ref, rows_hbm, out_ref, rows_ref, x_ref, sems):
    parts, local, tokens, width = x_ref.shape
    experts = code_ref.shape[1]
    part_rows = rows_ref.shape[0] // parts
    loads = []
    for part in range(parts):
        at = pl.ds(part * part_rows, part_rows)
        loads.append(pltpu.make_async_copy(rows_hbm.at[at], rows_ref.at[at], sems.at[part]))
        loads[-1].start()
    order, unused = block_orders(local)
    at = iota((1, local * tokens), 1)
    slot = (at % CAP).astype(F32)
    owner = (at % tokens) // CAP * local + at // tokens
    total = hidden_ref[...].astype(F32)
    for part in range(parts):
        first = part * (tokens // CAP) * local
        spread = (owner + first == iota((experts, local * tokens), 0)).astype(BF16)
        both = dot_nn(code_ref[...], spread)
        weights = jnp.where(both[:TOK] == slot, both[TOK:], 0.0).astype(BF16)
        loads[part].wait()
        count = part_rows // (local * GROUP_ROWS)
        unpack_blocks(order, rows_ref, part * part_rows, count, local, x_ref.at[part])
        total = total + dot_nn(weights, x_ref[part].reshape(local * tokens, width))
    out_ref[...] = total.astype(BF16)


def combine_call(code, rows, hidden, local):
    parts = COMBINE_PARTS
    tokens = rows.shape[0] // (parts * local * GROUPS)
    return pl.pallas_call(
        combine_kernel,
        in_specs=[pl.BlockSpec(memory_space=pltpu.VMEM)] * 2
        + [pl.BlockSpec(memory_space=pl.ANY)],
        out_specs=pl.BlockSpec(memory_space=pltpu.VMEM),
        out_shape=jax.ShapeDtypeStruct((TOK, D), BF16),
        scratch_shapes=[
            pltpu.VMEM(rows.shape, BF16),
            pltpu.VMEM((parts, local, tokens, D), BF16),
            pltpu.SemaphoreType.DMA((parts,)),
        ],
        compiler_params=params(),
        name="combine",
    )(code, hidden, rows)


def exchange(rows, axes, groups=None):
    return lax.all_to_all(
        rows, axes, split_axis=0, concat_axis=0, tiled=True, axis_index_groups=groups
    )


def per_device(
    queries,
    key_in,
    value_in,
    gate_in,
    residual_in,
    log_decay,
    beta_logit,
    lengths,
    head_gain,
    out_proj,
    post_gain,
    expert_in,
    expert_out,
    routes,
    route_gates,
):
    devices = lax.axis_size("dp") * lax.axis_size("ctx")
    local = expert_in.shape[0]
    shared = (key_in[0], value_in[0], log_decay[0], beta_logit[0])
    maps, solve = maps_call(lengths, *shared)
    query, inside = reads_call(lengths, queries[0], *shared, solve)
    code, code_t = route_call(routes[0].T, route_gates[0].T, local * devices)
    blocks = lax.axis_size("ctx")
    cores = [list(range(core, blocks, 2)) for core in range(2)]
    own = exchange(maps, "ctx", cores)
    other = lax.ppermute(own, "ctx", [(i, i ^ 1) for i in range(blocks)])
    states = exchange(scan_call(own, other), "ctx", cores)
    hidden, sent = finish_call(
        states,
        query,
        inside,
        gate_in[0],
        residual_in[0],
        head_gain[None],
        post_gain[None],
        code_t,
        out_proj,
    )
    both = ("dp", "ctx")
    arrived = exchange(sent.reshape(devices, local * SPAN, WIDTH), both)
    results = expert_call(arrived.reshape(sent.shape), expert_in, expert_out)
    returned = exchange(results.reshape(devices, local * SPAN, WIDTH), both)
    return combine_call(code, returned.reshape(sent.shape), hidden, local)[None]


def solution(mesh):
    tokens = P("dp", "ctx", None)
    heads = P("dp", None, "ctx")
    experts = P(("dp", "ctx"), None, None)
    in_specs = (tokens,) * 5 + (heads, heads, P("dp", None), P(), P(), P())
    in_specs += (experts, experts, tokens, tokens)
    return jax.shard_map(
        per_device, mesh=mesh, in_specs=in_specs, out_specs=tokens, check_vma=False
    )
```

```python
import jax
import jax.numpy as jnp
from jax import lax
from jax.experimental import pallas as pl
from jax.experimental.pallas import tpu as pltpu
from jax.sharding import PartitionSpec as P

D = 2048
DK = 128
DV = 128
FF = 512
TOPK = 10
HK = 8
HV = 16
TOK = 128
CAP = 6
GROUPS = 4
WIDTH = D // GROUPS
SPAN = GROUPS * CAP
EPSILON = 1e-06

F32 = jnp.float32
BF16 = jnp.bfloat16
HEADS_STEP = 16
MAP_ROWS = DV + DK + 16
SRC_GROUP = 4
GROUP_ROWS = SRC_GROUP * SPAN
PIECE = SRC_GROUP * CAP
DISPATCH_STEPS = 8
COMBINE_PARTS = 2
MIB = 1 << 20


def dot_nn(a, b):
    return lax.dot_general(a, b, (((1,), (0,)), ((), ())), preferred_element_type=F32)


def dot_nt(a, b):
    return lax.dot_general(a, b, (((1,), (1,)), ((), ())), preferred_element_type=F32)


def halves(x):
    high = x.astype(BF16)
    return high, (x - high.astype(F32)).astype(BF16)


def wide(x):
    high, low = halves(x)
    return jnp.concatenate([high, low], axis=1)


def twice(x, axis):
    return jnp.concatenate([x, x], axis=axis)


def iota(shape, axis):
    return lax.broadcasted_iota(jnp.int32, shape, axis)


def params(limit=60 * MIB):
    return pltpu.CompilerParams(vmem_limit_bytes=limit)


def block_frame(len_ref, k_ref, decay_ref, beta_ref):
    first = lax.axis_index("ctx") * TOK
    start1 = len_ref[0, 0]
    start2 = start1 + len_ref[0, 1]
    start3 = start2 + len_ref[0, 2]

    def segment(at):
        return (
            (at >= 0).astype(jnp.int32)
            + (at >= start1).astype(jnp.int32)
            + (at >= start2).astype(jnp.int32)
            + (at >= start3).astype(jnp.int32)
        )

    square = (TOK, TOK)
    rows, cols = iota(square, 0), iota(square, 1)
    seg_before, seg_last = segment(first - 1), segment(first + TOK - 1)
    lower = (segment(first + rows) == segment(first + cols)) & (rows >= cols)
    cum_row = lax.dot_general(
        decay_ref[...],
        (rows <= cols).astype(F32),
        (((1,), (0,)), ((), ())),
        precision=lax.Precision.HIGHEST,
        preferred_element_type=F32,
    )
    beta_row = 1.0 / (1.0 + jnp.exp(-beta_ref[...]))
    columns = jnp.concatenate(
        [cum_row, beta_row, jnp.zeros((TOK - 2 * HEADS_STEP, TOK), F32)], axis=0
    ).T
    row8 = iota((HEADS_STEP, TOK), 1)
    enter_row = jnp.where(segment(first + row8) == seg_before, jnp.exp(cum_row), 0.0)
    at = first + iota((TOK, 1), 0)
    enters, leaves = segment(at) == seg_before, segment(at) == seg_last
    cum_col = [columns[:, h : h + 1] for h in range(HEADS_STEP)]
    beta_col = [columns[:, HEADS_STEP + h : HEADS_STEP + h + 1] for h in range(HEADS_STEP)]
    key = [k_ref[:, i * DK : (i + 1) * DK] for i in range(HEADS_STEP // 2)]
    inner = [dot_nt(k, k) for k in key]
    squares = [jnp.where(rows == cols, x, 0.0) for x in inner]
    key_row = [lax.rsqrt(jnp.sum(x, 0, keepdims=True) + EPSILON) for x in squares]
    key_col = [lax.rsqrt(jnp.sum(x, 1, keepdims=True) + EPSILON) for x in squares]
    decay = [
        jnp.where(
            lower, jnp.exp(jnp.minimum(cum_col[h] - cum_row[h : h + 1], 0.0)), 0.0
        )
        for h in range(HEADS_STEP)
    ]
    rows_of = (beta_row, enter_row, key_row)
    columns_of = (cum_col, beta_col, key_col, enters, leaves)
    return rows, cols, key, inner, decay, rows_of, columns_of


def maps_kernel(len_ref, k_ref, v_ref, decay_ref, beta_ref, maps_ref, solve_ref):
    rows, cols, key, inner, decay, rows_of, columns_of = block_frame(
        len_ref, k_ref, decay_ref, beta_ref
    )
    beta_row, enter_row, key_row = rows_of
    cum_col, beta_col, key_col, enters, leaves = columns_of
    square = (TOK, TOK)
    heads = range(HEADS_STEP)
    strict = rows > cols
    eye = (rows == cols).astype(F32)
    inner = [x * r for x, r in zip(inner, key_row)]
    system = [
        jnp.where(strict, (beta_col[h] * key_col[h // 2]) * decay[h] * inner[h // 2], 0.0)
        for h in heads
    ]
    system_bf = [x.astype(BF16) for x in system]
    zero_bf = jnp.zeros(square, BF16)
    inverse = [eye.astype(BF16)] * HEADS_STEP
    size = 1
    while size < TOK:
        mask = (rows // (2 * size) == cols // (2 * size)) & (rows // size != cols // size)
        inside = [jnp.where(mask, x, zero_bf) for x in system_bf]
        if size > 1:
            inside = [dot_nn(x, y).astype(BF16) for x, y in zip(inside, inverse)]
            inside = [dot_nn(y, x).astype(BF16) for x, y in zip(inside, inverse)]
        inverse = [y - x for x, y in zip(inside, inverse)]
        size *= 2
    residual = [
        (eye - inverse[h].astype(F32) - dot_nn(wide(system[h]), twice(inverse[h], 0))).astype(BF16)
        for h in heads
    ]
    solve = [inverse[h].astype(F32) + dot_nn(inverse[h], residual[h]) for h in heads]
    for h in heads:
        solve_ref[h] = solve[h]

    key_pair = [twice(k, 0) for k in key]
    key_t_pair = [twice(k.T, 1) for k in key]
    value_t = [v_ref[:, h * DV : (h + 1) * DV].T for h in heads]
    weight_row = [beta_row[h : h + 1] * enter_row[h : h + 1] * key_row[h // 2] for h in heads]
    leave_col = [
        jnp.where(leaves, jnp.exp(jnp.minimum(cum_col[h][TOK - 1 :] - cum_col[h], 0.0)), 0.0)
        * key_col[h // 2]
        for h in heads
    ]
    left = [leave_col[h] * solve[h] for h in heads]
    offset_in = [dot_nt(twice(value_t[h], 1), wide(left[h] * beta_row[h : h + 1])) for h in heads]
    change_in = [dot_nt(key_t_pair[h // 2], wide(left[h] * weight_row[h])) for h in heads]
    offset = [dot_nn(wide(offset_in[h]), key_pair[h // 2]).astype(BF16) for h in heads]
    change = [dot_nn(wide(change_in[h]), key_pair[h // 2]).astype(BF16) for h in heads]
    at_row = iota((16, TOK), 0)
    for h in heads:
        keep = jnp.broadcast_to(enter_row[h : h + 1, TOK - 1 :], (16, TOK))
        keep_high = keep.astype(BF16)
        keep_mid, keep_low = halves(keep - keep_high.astype(F32))
        terms = jnp.where(
            at_row == 0,
            keep_high.astype(F32),
            jnp.where(
                at_row == 1,
                keep_mid.astype(F32),
                jnp.where(at_row == 2, keep_low.astype(F32), 0.0),
            ),
        ).astype(BF16)
        maps_ref[h, 0:DV, :] = offset[h]
        maps_ref[h, DV : DV + DK, :] = change[h]
        maps_ref[h, DV + DK :, :] = terms


def reads_kernel(
    len_ref, q_ref, k_ref, v_ref, decay_ref, beta_ref, solve_ref, query_ref, local_ref
):
    rows, cols, key, inner, decay, rows_of, columns_of = block_frame(
        len_ref, k_ref, decay_ref, beta_ref
    )
    beta_row, enter_row, key_row = rows_of
    cum_col, beta_col, key_col, enters, leaves = columns_of
    heads = range(HEADS_STEP)
    query = [q_ref[:, i * DK : (i + 1) * DK] for i in range(HEADS_STEP // 2)]
    query_f = [q.astype(F32) for q in query]
    query_col = [
        lax.rsqrt(jnp.sum(q * q, 1, keepdims=True) + EPSILON) * (DK**-0.5) for q in query_f
    ]
    cross = [dot_nt(q, k) * r * c for q, k, r, c in zip(query, key, key_row, query_col)]
    key_pair = [twice(k, 0) for k in key]
    value = [v_ref[:, h * DV : (h + 1) * DV] for h in heads]
    weight_row = [beta_row[h : h + 1] * enter_row[h : h + 1] * key_row[h // 2] for h in heads]
    mixed = []
    for h in heads:
        score_high, score_low = halves(decay[h] * cross[h // 2])
        solve_high, solve_low = halves(solve_ref[h])
        mixed.append(
            dot_nn(
                jnp.concatenate([score_high, score_low, score_high], axis=1),
                jnp.concatenate([solve_high, solve_high, solve_low], axis=0),
            )
        )
    for h in heads:
        local_ref[:, h * DV : (h + 1) * DV] = dot_nn(
            wide(mixed[h] * beta_row[h : h + 1]), twice(value[h], 0)
        ).astype(BF16)
    for h in heads:
        enter_col = jnp.where(enters, jnp.exp(cum_col[h]), 0.0) * query_col[h // 2]
        read = dot_nn(wide(mixed[h] * weight_row[h]), key_pair[h // 2])
        query_ref[h] = (enter_col * query_f[h // 2] - read).astype(BF16)


STEPS = HV // HEADS_STEP
LENGTHS = pl.BlockSpec(memory_space=pltpu.SMEM)
KEY_BLOCK = pl.BlockSpec((TOK, HK * DK // STEPS), lambda i: (0, i))
VALUE_BLOCK = pl.BlockSpec((TOK, HV * DV // STEPS), lambda i: (0, i))
HEAD_BLOCK = pl.BlockSpec((HEADS_STEP, TOK), lambda i: (i, 0))
SQUARE_BLOCK = pl.BlockSpec((HEADS_STEP, TOK, TOK), lambda i: (i, 0, 0))


def maps_call(lengths, key_in, value_in, log_decay, beta_logit):
    return pl.pallas_call(
        maps_kernel,
        grid=(STEPS,),
        in_specs=[LENGTHS, KEY_BLOCK, VALUE_BLOCK, HEAD_BLOCK, HEAD_BLOCK],
        out_specs=[
            pl.BlockSpec((HEADS_STEP, MAP_ROWS, DK), lambda i: (i, 0, 0)),
            SQUARE_BLOCK,
        ],
        out_shape=[
            jax.ShapeDtypeStruct((HV, MAP_ROWS, DK), BF16),
            jax.ShapeDtypeStruct((HV, TOK, TOK), F32),
        ],
        compiler_params=params(),
        name="block_maps",
    )(lengths, key_in, value_in, log_decay, beta_logit)


def reads_call(lengths, queries, key_in, value_in, log_decay, beta_logit, solve):
    return pl.pallas_call(
        reads_kernel,
        grid=(STEPS,),
        in_specs=[
            LENGTHS,
            KEY_BLOCK,
            KEY_BLOCK,
            VALUE_BLOCK,
            HEAD_BLOCK,
            HEAD_BLOCK,
            SQUARE_BLOCK,
        ],
        out_specs=[SQUARE_BLOCK, VALUE_BLOCK],
        out_shape=[
            jax.ShapeDtypeStruct((HV, TOK, DK), BF16),
            jax.ShapeDtypeStruct((TOK, HV * DV), BF16),
        ],
        compiler_params=params(),
        name="block_reads",
    )(lengths, queries, key_in, value_in, log_decay, beta_logit, solve)


def scan_kernel(own_ref, other_ref, out_ref):
    chips = own_ref.shape[0]
    even = lax.axis_index("ctx") % 2 == 0
    state = jnp.zeros((DV, DK), F32)
    for chip in range(chips):
        own, other = own_ref[chip], other_ref[chip]
        entering = []
        for block in (jnp.where(even, own, other), jnp.where(even, other, own)):
            high, low = halves(state)
            entering.append(high)
            keep = jnp.sum(block[DV + DK :].astype(F32), 0, keepdims=True)
            moved = dot_nn(jnp.concatenate([high, low], axis=0), block[DV : DV + DK])
            state = keep * state + block[:DV].astype(F32) - (moved[:DV] + moved[DV:])
        out_ref[chip * DV : (chip + 1) * DV, :] = jnp.where(even, entering[0], entering[1])


def scan_call(own, other):
    return pl.pallas_call(
        scan_kernel,
        out_shape=jax.ShapeDtypeStruct((own.shape[0] * DV, DK), BF16),
        compiler_params=params(24 * MIB),
        name="state_scan",
    )(own, other)


def finish_kernel(
    gain_ref,
    post_ref,
    code_ref,
    state_ref,
    query_ref,
    local_ref,
    gate_ref,
    resid_ref,
    weight_ref,
    hidden_ref,
    out_ref,
    rows_ref,
):
    gain = gain_ref[...]
    normed = []
    for h in range(HV):
        cut = slice(h * DV, (h + 1) * DV)
        outputs = local_ref[:, cut].astype(F32) + dot_nt(query_ref[h], state_ref[cut, :])
        scale = lax.rsqrt(jnp.mean(outputs * outputs, -1, keepdims=True) + EPSILON)
        gate = gate_ref[:, cut].astype(F32)
        normed.append((outputs * scale * gain * (gate / (1.0 + jnp.exp(-gate)))).astype(BF16))
    normed = jnp.concatenate(normed, axis=1)
    total = jnp.zeros((TOK, 1), F32)
    parts = []
    for g in range(GROUPS):
        cut = slice(g * WIDTH, (g + 1) * WIDTH)
        mixed = dot_nn(normed, weight_ref[:, cut])
        hidden = (resid_ref[:, cut].astype(F32) + mixed).astype(BF16)
        hidden_ref[:, cut] = hidden
        hidden = hidden.astype(F32)
        total = total + jnp.sum(hidden * hidden, -1, keepdims=True)
        parts.append(hidden)
    scale = lax.rsqrt(total / D + EPSILON)
    for g in range(GROUPS):
        cut = slice(g * WIDTH, (g + 1) * WIDTH)
        rows_ref[g * TOK : (g + 1) * TOK, :] = (parts[g] * scale * post_ref[:, cut]).astype(BF16)

    count = code_ref.shape[0] // DISPATCH_STEPS
    for step in range(DISPATCH_STEPS):
        code = code_ref[step * count : (step + 1) * count, :][:, None, :]
        tiles = []
        for part in range(SPAN // 8):
            at = iota((1, 8, TOK), 1) + 8 * part
            slot, group = at % CAP, at // CAP
            pick = [
                jnp.where(code == jnp.where(group == g, slot, TOK).astype(F32), 1.0, 0.0)
                .reshape(count * 8, TOK)
                .astype(BF16)
                for g in (part, part + 1)
            ]
            source = rows_ref[part * TOK : (part + 2) * TOK, :]
            tiles.append(dot_nn(jnp.concatenate(pick, axis=1), source).reshape(count, 1, 8, WIDTH))
        at = pl.ds(step * count * SPAN, count * SPAN)
        out_ref[at, :] = jnp.concatenate(tiles, axis=1).reshape(count * SPAN, WIDTH).astype(BF16)


def finish_call(state, query, local, gate_in, residual_in, head_gain, post_gain, code_t, out_proj):
    experts = code_t.shape[0]
    hidden = jax.ShapeDtypeStruct((TOK, D), BF16)
    sent = jax.ShapeDtypeStruct((experts * SPAN, WIDTH), BF16)
    rows = jax.ShapeDtypeStruct((GROUPS * TOK, WIDTH), BF16)
    return pl.pallas_call(
        finish_kernel,
        in_specs=[pl.BlockSpec(memory_space=pltpu.VMEM)] * 9,
        out_specs=[pl.BlockSpec(memory_space=pltpu.VMEM)] * 2,
        out_shape=[hidden, sent],
        scratch_shapes=[pltpu.VMEM(rows.shape, BF16)],
        compiler_params=params(24 * MIB),
        name="mixer_finish",
    )(
        head_gain, post_gain, code_t, state, query, local, gate_in, residual_in, out_proj
    )


def route_kernel(routes_ref, gates_ref, code_ref, code_t_ref):
    experts = code_t_ref.shape[0]
    expert = iota((experts, TOK), 0)
    hit = jnp.zeros((experts, TOK), F32)
    gate = jnp.zeros((experts, TOK), F32)
    for k in range(TOPK):
        match = routes_ref[k : k + 1, :] == expert
        hit = jnp.where(match, 1.0, hit)
        gate = jnp.where(match, gates_ref[k : k + 1, :], gate)
    square = (TOK, TOK)
    before = (iota(square, 0) < iota(square, 1)).astype(BF16)
    rank = dot_nn(hit.astype(BF16), before)
    code = jnp.where(hit > 0.0, rank, -1.0)
    code_t_ref[...] = code
    for at in range(0, experts, TOK):
        cut = slice(at, at + TOK)
        code_ref[0:TOK, cut] = code[cut].T.astype(BF16)
        code_ref[TOK:, cut] = gate[cut].T.astype(BF16)


def route_call(routes, gates, experts):
    return pl.pallas_call(
        route_kernel,
        out_shape=[
            jax.ShapeDtypeStruct((2 * TOK, experts), BF16),
            jax.ShapeDtypeStruct((experts, TOK), F32),
        ],
        compiler_params=params(),
        name="routing",
    )(routes, gates)


def block_orders(local):
    block_rows = local * GROUP_ROWS
    square = (block_rows, block_rows)
    to_at, from_at = iota(square, 0), iota(square, 1)

    def source_of(at):
        piece, rest = at // PIECE, at % PIECE
        return (rest // CAP) * (local * SPAN) + piece * CAP + rest % CAP

    order = (source_of(to_at) == from_at).astype(BF16)
    back = (source_of(from_at) == to_at).astype(BF16)
    return order, back


def unpack_blocks(order, rows_ref, base, count, local, x_ref):
    block_rows = local * GROUP_ROWS
    for i in range(0, count, 2):
        moved = [
            dot_nn(order, rows_ref[base + k * block_rows : base + (k + 1) * block_rows, :])
            for k in (i, i + 1)
        ]
        for j in range(local):
            for g in range(GROUPS):
                cut = slice((j * GROUPS + g) * PIECE, (j * GROUPS + g + 1) * PIECE)
                x_ref[j, i * PIECE : (i + 2) * PIECE, g * WIDTH : (g + 1) * WIDTH] = (
                    jnp.concatenate([m[cut] for m in moved], axis=0).astype(BF16)
                )


def expert_kernel(rows_ref, in_ref, out_ref, result_ref, x_ref, y_ref):
    local = in_ref.shape[0]
    half = rows_ref.shape[0] // 2
    block_rows = local * GROUP_ROWS
    count = half // block_rows
    order, back = block_orders(local)
    for part in range(2):
        base = part * half
        unpack_blocks(order, rows_ref, base, count, local, x_ref)
        for j in range(local):
            x = x_ref[j]
            gate = dot_nn(x, in_ref[j, :, :FF])
            up = dot_nn(x, in_ref[j, :, FF:])
            hidden = (gate / (1.0 + jnp.exp(-gate)) * up).astype(BF16)
            y_ref[j] = dot_nn(hidden, out_ref[j])
        for i in range(count):
            block = jnp.concatenate(
                [
                    y_ref[j, i * PIECE : (i + 1) * PIECE, g * WIDTH : (g + 1) * WIDTH]
                    for j in range(local)
                    for g in range(GROUPS)
                ],
                axis=0,
            ).astype(BF16)
            at = pl.ds(base + i * block_rows, block_rows)
            result_ref[at, :] = dot_nn(back, block).astype(BF16)


def expert_call(rows, expert_in, expert_out):
    total = rows.shape[0]
    local = expert_in.shape[0]
    tokens = total // (2 * GROUPS * local)
    return pl.pallas_call(
        expert_kernel,
        in_specs=[pl.BlockSpec(memory_space=pltpu.VMEM)] * 3,
        out_specs=pl.BlockSpec(memory_space=pltpu.VMEM),
        out_shape=jax.ShapeDtypeStruct((total, WIDTH), BF16),
        scratch_shapes=[
            pltpu.VMEM((local, tokens, D), BF16),
            pltpu.VMEM((local, tokens, D), F32),
        ],
        compiler_params=params(28 * MIB),
        name="experts",
    )(rows, expert_in, expert_out)


def combine_kernel(code_ref, hidden_ref, rows_ref, out_ref, x_ref):
    parts, local, tokens, width = x_ref.shape
    experts = code_ref.shape[1]
    part_rows = rows_ref.shape[0] // parts
    order, unused = block_orders(local)
    at = iota((1, local * tokens), 1)
    slot = (at % CAP).astype(F32)
    owner = (at % tokens) // CAP * local + at // tokens
    total = hidden_ref[...].astype(F32)
    for part in range(parts):
        first = part * (tokens // CAP) * local
        spread = (owner + first == iota((experts, local * tokens), 0)).astype(BF16)
        both = dot_nn(code_ref[...], spread)
        weights = jnp.where(both[:TOK] == slot, both[TOK:], 0.0).astype(BF16)
        count = part_rows // (local * GROUP_ROWS)
        unpack_blocks(order, rows_ref, part * part_rows, count, local, x_ref.at[part])
        total = total + dot_nn(weights, x_ref[part].reshape(local * tokens, width))
    out_ref[...] = total.astype(BF16)


def combine_call(code, rows, hidden, local):
    parts = COMBINE_PARTS
    tokens = rows.shape[0] // (parts * local * GROUPS)
    return pl.pallas_call(
        combine_kernel,
        in_specs=[pl.BlockSpec(memory_space=pltpu.VMEM)] * 3,
        out_specs=pl.BlockSpec(memory_space=pltpu.VMEM),
        out_shape=jax.ShapeDtypeStruct((TOK, D), BF16),
        scratch_shapes=[
            pltpu.VMEM((parts, local, tokens, D), BF16),
        ],
        compiler_params=params(32 * MIB),
        name="combine",
    )(code, hidden, rows)


def exchange(rows, axes, groups=None):
    return lax.all_to_all(
        rows, axes, split_axis=0, concat_axis=0, tiled=True, axis_index_groups=groups
    )


def per_device(
    queries,
    key_in,
    value_in,
    gate_in,
    residual_in,
    log_decay,
    beta_logit,
    lengths,
    head_gain,
    out_proj,
    post_gain,
    expert_in,
    expert_out,
    routes,
    route_gates,
):
    devices = lax.axis_size("dp") * lax.axis_size("ctx")
    local = expert_in.shape[0]
    shared = (key_in[0], value_in[0], log_decay[0], beta_logit[0])
    maps, solve = maps_call(lengths, *shared)
    query, inside = reads_call(lengths, queries[0], *shared, solve)
    code, code_t = route_call(routes[0].T, route_gates[0].T, local * devices)
    blocks = lax.axis_size("ctx")
    cores = [list(range(core, blocks, 2)) for core in range(2)]
    own = exchange(maps, "ctx", cores)
    own, query, inside, code, code_t = lax.optimization_barrier(
        (own, query, inside, code, code_t)
    )
    other = lax.ppermute(own, "ctx", [(i, i ^ 1) for i in range(blocks)])
    states = exchange(scan_call(own, other), "ctx", cores)
    hidden, sent = finish_call(
        states,
        query,
        inside,
        gate_in[0],
        residual_in[0],
        head_gain[None],
        post_gain[None],
        code_t,
        out_proj,
    )
    both = ("dp", "ctx")
    arrived = exchange(sent.reshape(devices, local * SPAN, WIDTH), both)
    results = expert_call(arrived.reshape(sent.shape), expert_in, expert_out)
    returned = exchange(results.reshape(devices, local * SPAN, WIDTH), both)
    return combine_call(code, returned.reshape(sent.shape), hidden, local)[None]


def solution(mesh):
    tokens = P("dp", "ctx", None)
    heads = P("dp", None, "ctx")
    experts = P(("dp", "ctx"), None, None)
    in_specs = (tokens,) * 5 + (heads, heads, P("dp", None), P(), P(), P())
    in_specs += (experts, experts, tokens, tokens)
    return jax.shard_map(
        per_device, mesh=mesh, in_specs=in_specs, out_specs=tokens, check_vma=False
    )
```

```python
import jax
import jax.numpy as jnp
from jax import lax
from jax.experimental import pallas as pl
from jax.experimental.pallas import tpu as pltpu
from jax.sharding import PartitionSpec as P

D = 2048
DK = 128
DV = 128
FF = 512
TOPK = 10
HK = 8
HV = 16
TOK = 128
CAP = 6
GROUPS = 4
WIDTH = D // GROUPS
SPAN = GROUPS * CAP
EPSILON = 1e-06

F32 = jnp.float32
BF16 = jnp.bfloat16
HEADS_STEP = 16
MAP_ROWS = DV + DK + 16
SRC_GROUP = 4
GROUP_ROWS = SRC_GROUP * SPAN
PIECE = SRC_GROUP * CAP
DISPATCH_STEPS = 8
COMBINE_PARTS = 2
MIB = 1 << 20


def dot_nn(a, b):
    return lax.dot_general(a, b, (((1,), (0,)), ((), ())), preferred_element_type=F32)


def dot_nt(a, b):
    return lax.dot_general(a, b, (((1,), (1,)), ((), ())), preferred_element_type=F32)


def halves(x):
    high = x.astype(BF16)
    return high, (x - high.astype(F32)).astype(BF16)


def wide(x):
    high, low = halves(x)
    return jnp.concatenate([high, low], axis=1)


def twice(x, axis):
    return jnp.concatenate([x, x], axis=axis)


def iota(shape, axis):
    return lax.broadcasted_iota(jnp.int32, shape, axis)


def params(limit=60 * MIB):
    return pltpu.CompilerParams(vmem_limit_bytes=limit)


def block_frame(len_ref, k_ref, decay_ref, beta_ref):
    first = lax.axis_index("ctx") * TOK
    start1 = len_ref[0, 0]
    start2 = start1 + len_ref[0, 1]
    start3 = start2 + len_ref[0, 2]

    def segment(at):
        return (
            (at >= 0).astype(jnp.int32)
            + (at >= start1).astype(jnp.int32)
            + (at >= start2).astype(jnp.int32)
            + (at >= start3).astype(jnp.int32)
        )

    square = (TOK, TOK)
    rows, cols = iota(square, 0), iota(square, 1)
    seg_before, seg_last = segment(first - 1), segment(first + TOK - 1)
    lower = (segment(first + rows) == segment(first + cols)) & (rows >= cols)
    cum_row = lax.dot_general(
        decay_ref[...],
        (rows <= cols).astype(F32),
        (((1,), (0,)), ((), ())),
        precision=lax.Precision.HIGHEST,
        preferred_element_type=F32,
    )
    beta_row = 1.0 / (1.0 + jnp.exp(-beta_ref[...]))
    columns = jnp.concatenate(
        [cum_row, beta_row, jnp.zeros((TOK - 2 * HEADS_STEP, TOK), F32)], axis=0
    ).T
    row8 = iota((HEADS_STEP, TOK), 1)
    enter_row = jnp.where(segment(first + row8) == seg_before, jnp.exp(cum_row), 0.0)
    at = first + iota((TOK, 1), 0)
    enters, leaves = segment(at) == seg_before, segment(at) == seg_last
    cum_col = [columns[:, h : h + 1] for h in range(HEADS_STEP)]
    beta_col = [columns[:, HEADS_STEP + h : HEADS_STEP + h + 1] for h in range(HEADS_STEP)]
    key = [k_ref[:, i * DK : (i + 1) * DK] for i in range(HEADS_STEP // 2)]
    inner = [dot_nt(k, k) for k in key]
    squares = [jnp.where(rows == cols, x, 0.0) for x in inner]
    key_row = [lax.rsqrt(jnp.sum(x, 0, keepdims=True) + EPSILON) for x in squares]
    key_col = [lax.rsqrt(jnp.sum(x, 1, keepdims=True) + EPSILON) for x in squares]
    decay = [
        jnp.where(
            lower, jnp.exp(jnp.minimum(cum_col[h] - cum_row[h : h + 1], 0.0)), 0.0
        )
        for h in range(HEADS_STEP)
    ]
    rows_of = (beta_row, enter_row, key_row)
    columns_of = (cum_col, beta_col, key_col, enters, leaves)
    return rows, cols, key, inner, decay, rows_of, columns_of


def maps_kernel(len_ref, k_ref, v_ref, decay_ref, beta_ref, maps_ref, solve_ref):
    rows, cols, key, inner, decay, rows_of, columns_of = block_frame(
        len_ref, k_ref, decay_ref, beta_ref
    )
    beta_row, enter_row, key_row = rows_of
    cum_col, beta_col, key_col, enters, leaves = columns_of
    square = (TOK, TOK)
    heads = range(HEADS_STEP)
    strict = rows > cols
    eye = (rows == cols).astype(F32)
    inner = [x * r for x, r in zip(inner, key_row)]
    system = [
        jnp.where(strict, (beta_col[h] * key_col[h // 2]) * decay[h] * inner[h // 2], 0.0)
        for h in heads
    ]
    system_bf = [x.astype(BF16) for x in system]
    zero_bf = jnp.zeros(square, BF16)
    inverse = [eye.astype(BF16)] * HEADS_STEP
    size = 1
    while size < TOK:
        mask = (rows // (2 * size) == cols // (2 * size)) & (rows // size != cols // size)
        inside = [jnp.where(mask, x, zero_bf) for x in system_bf]
        if size > 1:
            inside = [dot_nn(x, y).astype(BF16) for x, y in zip(inside, inverse)]
            inside = [dot_nn(y, x).astype(BF16) for x, y in zip(inside, inverse)]
        inverse = [y - x for x, y in zip(inside, inverse)]
        size *= 2
    residual = [
        (eye - inverse[h].astype(F32) - dot_nn(wide(system[h]), twice(inverse[h], 0))).astype(BF16)
        for h in heads
    ]
    solve = [inverse[h].astype(F32) + dot_nn(inverse[h], residual[h]) for h in heads]
    for h in heads:
        solve_ref[h] = solve[h]

    key_pair = [twice(k, 0) for k in key]
    key_t_pair = [twice(k.T, 1) for k in key]
    value_t = [v_ref[:, h * DV : (h + 1) * DV].T for h in heads]
    weight_row = [beta_row[h : h + 1] * enter_row[h : h + 1] * key_row[h // 2] for h in heads]
    leave_col = [
        jnp.where(leaves, jnp.exp(jnp.minimum(cum_col[h][TOK - 1 :] - cum_col[h], 0.0)), 0.0)
        * key_col[h // 2]
        for h in heads
    ]
    left = [leave_col[h] * solve[h] for h in heads]
    offset_in = [dot_nt(twice(value_t[h], 1), wide(left[h] * beta_row[h : h + 1])) for h in heads]
    change_in = [dot_nt(key_t_pair[h // 2], wide(left[h] * weight_row[h])) for h in heads]
    offset = [dot_nn(wide(offset_in[h]), key_pair[h // 2]).astype(BF16) for h in heads]
    change = [dot_nn(wide(change_in[h]), key_pair[h // 2]).astype(BF16) for h in heads]
    at_row = iota((16, TOK), 0)
    for h in heads:
        keep = jnp.broadcast_to(enter_row[h : h + 1, TOK - 1 :], (16, TOK))
        keep_high = keep.astype(BF16)
        keep_mid, keep_low = halves(keep - keep_high.astype(F32))
        terms = jnp.where(
            at_row == 0,
            keep_high.astype(F32),
            jnp.where(
                at_row == 1,
                keep_mid.astype(F32),
                jnp.where(at_row == 2, keep_low.astype(F32), 0.0),
            ),
        ).astype(BF16)
        maps_ref[h, 0:DV, :] = offset[h]
        maps_ref[h, DV : DV + DK, :] = change[h]
        maps_ref[h, DV + DK :, :] = terms


def reads_kernel(
    len_ref, q_ref, k_ref, v_ref, decay_ref, beta_ref, solve_ref, query_ref, local_ref
):
    rows, cols, key, inner, decay, rows_of, columns_of = block_frame(
        len_ref, k_ref, decay_ref, beta_ref
    )
    beta_row, enter_row, key_row = rows_of
    cum_col, beta_col, key_col, enters, leaves = columns_of
    heads = range(HEADS_STEP)
    query = [q_ref[:, i * DK : (i + 1) * DK] for i in range(HEADS_STEP // 2)]
    query_f = [q.astype(F32) for q in query]
    query_col = [
        lax.rsqrt(jnp.sum(q * q, 1, keepdims=True) + EPSILON) * (DK**-0.5) for q in query_f
    ]
    cross = [dot_nt(q, k) * r * c for q, k, r, c in zip(query, key, key_row, query_col)]
    key_pair = [twice(k, 0) for k in key]
    value = [v_ref[:, h * DV : (h + 1) * DV] for h in heads]
    weight_row = [beta_row[h : h + 1] * enter_row[h : h + 1] * key_row[h // 2] for h in heads]
    mixed = []
    for h in heads:
        score_high, score_low = halves(decay[h] * cross[h // 2])
        solve_high, solve_low = halves(solve_ref[h])
        mixed.append(
            dot_nn(
                jnp.concatenate([score_high, score_low, score_high], axis=1),
                jnp.concatenate([solve_high, solve_high, solve_low], axis=0),
            )
        )
    for h in heads:
        local_ref[:, h * DV : (h + 1) * DV] = dot_nn(
            wide(mixed[h] * beta_row[h : h + 1]), twice(value[h], 0)
        ).astype(BF16)
    for h in heads:
        enter_col = jnp.where(enters, jnp.exp(cum_col[h]), 0.0) * query_col[h // 2]
        read = dot_nn(wide(mixed[h] * weight_row[h]), key_pair[h // 2])
        query_ref[h] = (enter_col * query_f[h // 2] - read).astype(BF16)


STEPS = HV // HEADS_STEP
LENGTHS = pl.BlockSpec(memory_space=pltpu.SMEM)
KEY_BLOCK = pl.BlockSpec((TOK, HK * DK // STEPS), lambda i: (0, i))
VALUE_BLOCK = pl.BlockSpec((TOK, HV * DV // STEPS), lambda i: (0, i))
HEAD_BLOCK = pl.BlockSpec((HEADS_STEP, TOK), lambda i: (i, 0))
SQUARE_BLOCK = pl.BlockSpec((HEADS_STEP, TOK, TOK), lambda i: (i, 0, 0))


def maps_call(lengths, key_in, value_in, log_decay, beta_logit):
    return pl.pallas_call(
        maps_kernel,
        grid=(STEPS,),
        in_specs=[LENGTHS, KEY_BLOCK, VALUE_BLOCK, HEAD_BLOCK, HEAD_BLOCK],
        out_specs=[
            pl.BlockSpec((HEADS_STEP, MAP_ROWS, DK), lambda i: (i, 0, 0)),
            SQUARE_BLOCK,
        ],
        out_shape=[
            jax.ShapeDtypeStruct((HV, MAP_ROWS, DK), BF16),
            jax.ShapeDtypeStruct((HV, TOK, TOK), F32),
        ],
        compiler_params=params(),
        name="block_maps",
    )(lengths, key_in, value_in, log_decay, beta_logit)


def reads_call(lengths, queries, key_in, value_in, log_decay, beta_logit, solve):
    return pl.pallas_call(
        reads_kernel,
        grid=(STEPS,),
        in_specs=[
            LENGTHS,
            KEY_BLOCK,
            KEY_BLOCK,
            VALUE_BLOCK,
            HEAD_BLOCK,
            HEAD_BLOCK,
            SQUARE_BLOCK,
        ],
        out_specs=[SQUARE_BLOCK, VALUE_BLOCK],
        out_shape=[
            jax.ShapeDtypeStruct((HV, TOK, DK), BF16),
            jax.ShapeDtypeStruct((TOK, HV * DV), BF16),
        ],
        compiler_params=params(),
        name="block_reads",
    )(lengths, queries, key_in, value_in, log_decay, beta_logit, solve)


def scan_kernel(own_ref, other_ref, out_ref):
    chips = own_ref.shape[0]
    even = lax.axis_index("ctx") % 2 == 0
    state = jnp.zeros((DV, DK), F32)
    for chip in range(chips):
        own, other = own_ref[chip], other_ref[chip]
        entering = []
        for block in (jnp.where(even, own, other), jnp.where(even, other, own)):
            high, low = halves(state)
            entering.append(high)
            keep = jnp.sum(block[DV + DK :].astype(F32), 0, keepdims=True)
            moved = dot_nn(jnp.concatenate([high, low], axis=0), block[DV : DV + DK])
            state = keep * state + block[:DV].astype(F32) - (moved[:DV] + moved[DV:])
        out_ref[chip * DV : (chip + 1) * DV, :] = jnp.where(even, entering[0], entering[1])


def scan_call(own, other):
    return pl.pallas_call(
        scan_kernel,
        out_shape=jax.ShapeDtypeStruct((own.shape[0] * DV, DK), BF16),
        compiler_params=params(24 * MIB),
        cost_estimate=pl.CostEstimate(
            flops=6 * 10**9, bytes_accessed=4 * 10**6, transcendentals=0
        ),
        name="state_scan",
    )(own, other)


def finish_kernel(
    gain_ref,
    post_ref,
    code_ref,
    state_ref,
    weight_ref,
    query_hbm,
    local_hbm,
    gate_hbm,
    resid_hbm,
    hidden_ref,
    out_ref,
    rows_ref,
    query_ref,
    local_ref,
    gate_ref,
    resid_ref,
    sems,
):
    loads = [
        pltpu.make_async_copy(source, target, sems.at[i])
        for i, (source, target) in enumerate(
            [
                (query_hbm, query_ref),
                (local_hbm, local_ref),
                (gate_hbm, gate_ref),
                (resid_hbm, resid_ref),
            ]
        )
    ]
    for load in loads:
        load.start()
    for load in loads:
        load.wait()
    gain = gain_ref[...]
    normed = []
    for h in range(HV):
        cut = slice(h * DV, (h + 1) * DV)
        outputs = local_ref[:, cut].astype(F32) + dot_nt(query_ref[h], state_ref[cut, :])
        scale = lax.rsqrt(jnp.mean(outputs * outputs, -1, keepdims=True) + EPSILON)
        gate = gate_ref[:, cut].astype(F32)
        normed.append((outputs * scale * gain * (gate / (1.0 + jnp.exp(-gate)))).astype(BF16))
    normed = jnp.concatenate(normed, axis=1)
    total = jnp.zeros((TOK, 1), F32)
    parts = []
    for g in range(GROUPS):
        cut = slice(g * WIDTH, (g + 1) * WIDTH)
        mixed = dot_nn(normed, weight_ref[:, cut])
        hidden = (resid_ref[:, cut].astype(F32) + mixed).astype(BF16)
        hidden_ref[:, cut] = hidden
        hidden = hidden.astype(F32)
        total = total + jnp.sum(hidden * hidden, -1, keepdims=True)
        parts.append(hidden)
    scale = lax.rsqrt(total / D + EPSILON)
    for g in range(GROUPS):
        cut = slice(g * WIDTH, (g + 1) * WIDTH)
        rows_ref[g * TOK : (g + 1) * TOK, :] = (parts[g] * scale * post_ref[:, cut]).astype(BF16)

    count = code_ref.shape[0] // DISPATCH_STEPS
    for step in range(DISPATCH_STEPS):
        code = code_ref[step * count : (step + 1) * count, :][:, None, :]
        tiles = []
        for part in range(SPAN // 8):
            at = iota((1, 8, TOK), 1) + 8 * part
            slot, group = at % CAP, at // CAP
            pick = [
                jnp.where(code == jnp.where(group == g, slot, TOK).astype(F32), 1.0, 0.0)
                .reshape(count * 8, TOK)
                .astype(BF16)
                for g in (part, part + 1)
            ]
            source = rows_ref[part * TOK : (part + 2) * TOK, :]
            tiles.append(dot_nn(jnp.concatenate(pick, axis=1), source).reshape(count, 1, 8, WIDTH))
        at = pl.ds(step * count * SPAN, count * SPAN)
        out_ref[at, :] = jnp.concatenate(tiles, axis=1).reshape(count * SPAN, WIDTH).astype(BF16)


def finish_call(state, query, local, gate_in, residual_in, head_gain, post_gain, code_t, out_proj):
    experts = code_t.shape[0]
    hidden = jax.ShapeDtypeStruct((TOK, D), BF16)
    sent = jax.ShapeDtypeStruct((experts * SPAN, WIDTH), BF16)
    rows = jax.ShapeDtypeStruct((GROUPS * TOK, WIDTH), BF16)
    return pl.pallas_call(
        finish_kernel,
        in_specs=[pl.BlockSpec(memory_space=pltpu.VMEM)] * 5
        + [pl.BlockSpec(memory_space=pl.ANY)] * 4,
        out_specs=[pl.BlockSpec(memory_space=pltpu.VMEM)] * 2,
        out_shape=[hidden, sent],
        scratch_shapes=[
            pltpu.VMEM(x.shape, x.dtype) for x in [rows, query, local, gate_in, residual_in]
        ]
        + [pltpu.SemaphoreType.DMA((4,))],
        compiler_params=params(24 * MIB),
        name="mixer_finish",
    )(head_gain, post_gain, code_t, state, out_proj, query, local, gate_in, residual_in)


def route_kernel(routes_ref, gates_ref, code_ref, code_t_ref):
    experts = code_t_ref.shape[0]
    expert = iota((experts, TOK), 0)
    hit = jnp.zeros((experts, TOK), F32)
    gate = jnp.zeros((experts, TOK), F32)
    for k in range(TOPK):
        match = routes_ref[k : k + 1, :] == expert
        hit = jnp.where(match, 1.0, hit)
        gate = jnp.where(match, gates_ref[k : k + 1, :], gate)
    square = (TOK, TOK)
    before = (iota(square, 0) < iota(square, 1)).astype(BF16)
    rank = dot_nn(hit.astype(BF16), before)
    code = jnp.where(hit > 0.0, rank, -1.0)
    code_t_ref[...] = code
    for at in range(0, experts, TOK):
        cut = slice(at, at + TOK)
        code_ref[0:TOK, cut] = code[cut].T.astype(BF16)
        code_ref[TOK:, cut] = gate[cut].T.astype(BF16)


def route_call(routes, gates, experts):
    return pl.pallas_call(
        route_kernel,
        out_shape=[
            jax.ShapeDtypeStruct((2 * TOK, experts), BF16),
            jax.ShapeDtypeStruct((experts, TOK), F32),
        ],
        compiler_params=params(),
        name="routing",
    )(routes, gates)


def block_orders(local):
    block_rows = local * GROUP_ROWS
    square = (block_rows, block_rows)
    to_at, from_at = iota(square, 0), iota(square, 1)

    def source_of(at):
        piece, rest = at // PIECE, at % PIECE
        return (rest // CAP) * (local * SPAN) + piece * CAP + rest % CAP

    order = (source_of(to_at) == from_at).astype(BF16)
    back = (source_of(from_at) == to_at).astype(BF16)
    return order, back


def unpack_blocks(order, rows_ref, base, count, local, x_ref):
    block_rows = local * GROUP_ROWS
    for i in range(0, count, 2):
        moved = [
            dot_nn(order, rows_ref[base + k * block_rows : base + (k + 1) * block_rows, :])
            for k in (i, i + 1)
        ]
        for j in range(local):
            for g in range(GROUPS):
                cut = slice((j * GROUPS + g) * PIECE, (j * GROUPS + g + 1) * PIECE)
                x_ref[j, i * PIECE : (i + 2) * PIECE, g * WIDTH : (g + 1) * WIDTH] = (
                    jnp.concatenate([m[cut] for m in moved], axis=0).astype(BF16)
                )


def expert_kernel(rows_ref, in_ref, out_ref, result_ref, x_ref, y_ref):
    local = in_ref.shape[0]
    half = rows_ref.shape[0] // 2
    block_rows = local * GROUP_ROWS
    count = half // block_rows
    order, back = block_orders(local)
    for part in range(2):
        base = part * half
        unpack_blocks(order, rows_ref, base, count, local, x_ref)
        for j in range(local):
            x = x_ref[j]
            gate = dot_nn(x, in_ref[j, :, :FF])
            up = dot_nn(x, in_ref[j, :, FF:])
            hidden = (gate / (1.0 + jnp.exp(-gate)) * up).astype(BF16)
            y_ref[j] = dot_nn(hidden, out_ref[j])
        for i in range(count):
            block = jnp.concatenate(
                [
                    y_ref[j, i * PIECE : (i + 1) * PIECE, g * WIDTH : (g + 1) * WIDTH]
                    for j in range(local)
                    for g in range(GROUPS)
                ],
                axis=0,
            ).astype(BF16)
            at = pl.ds(base + i * block_rows, block_rows)
            result_ref[at, :] = dot_nn(back, block).astype(BF16)


def expert_call(rows, expert_in, expert_out):
    total = rows.shape[0]
    local = expert_in.shape[0]
    tokens = total // (2 * GROUPS * local)
    return pl.pallas_call(
        expert_kernel,
        in_specs=[pl.BlockSpec(memory_space=pltpu.VMEM)] * 3,
        out_specs=pl.BlockSpec(memory_space=pltpu.VMEM),
        out_shape=jax.ShapeDtypeStruct((total, WIDTH), BF16),
        scratch_shapes=[
            pltpu.VMEM((local, tokens, D), BF16),
            pltpu.VMEM((local, tokens, D), F32),
        ],
        compiler_params=params(28 * MIB),
        name="experts",
    )(rows, expert_in, expert_out)


def combine_kernel(code_ref, hidden_ref, rows_ref, out_ref, x_ref):
    parts, local, tokens, width = x_ref.shape
    experts = code_ref.shape[1]
    part_rows = rows_ref.shape[0] // parts
    order, unused = block_orders(local)
    at = iota((1, local * tokens), 1)
    slot = (at % CAP).astype(F32)
    owner = (at % tokens) // CAP * local + at // tokens
    total = hidden_ref[...].astype(F32)
    for part in range(parts):
        first = part * (tokens // CAP) * local
        spread = (owner + first == iota((experts, local * tokens), 0)).astype(BF16)
        both = dot_nn(code_ref[...], spread)
        weights = jnp.where(both[:TOK] == slot, both[TOK:], 0.0).astype(BF16)
        count = part_rows // (local * GROUP_ROWS)
        unpack_blocks(order, rows_ref, part * part_rows, count, local, x_ref.at[part])
        total = total + dot_nn(weights, x_ref[part].reshape(local * tokens, width))
    out_ref[...] = total.astype(BF16)


def combine_call(code, rows, hidden, local):
    parts = COMBINE_PARTS
    tokens = rows.shape[0] // (parts * local * GROUPS)
    return pl.pallas_call(
        combine_kernel,
        in_specs=[pl.BlockSpec(memory_space=pltpu.VMEM)] * 3,
        out_specs=pl.BlockSpec(memory_space=pltpu.VMEM),
        out_shape=jax.ShapeDtypeStruct((TOK, D), BF16),
        scratch_shapes=[
            pltpu.VMEM((parts, local, tokens, D), BF16),
        ],
        compiler_params=params(32 * MIB),
        name="combine",
    )(code, hidden, rows)


def exchange(rows, axes, groups=None):
    return lax.all_to_all(
        rows, axes, split_axis=0, concat_axis=0, tiled=True, axis_index_groups=groups
    )


def per_device(
    queries,
    key_in,
    value_in,
    gate_in,
    residual_in,
    log_decay,
    beta_logit,
    lengths,
    head_gain,
    out_proj,
    post_gain,
    expert_in,
    expert_out,
    routes,
    route_gates,
):
    devices = lax.axis_size("dp") * lax.axis_size("ctx")
    local = expert_in.shape[0]
    shared = (key_in[0], value_in[0], log_decay[0], beta_logit[0])
    maps, solve = maps_call(lengths, *shared)
    query, inside = reads_call(lengths, queries[0], *shared, solve)
    code, code_t = route_call(routes[0].T, route_gates[0].T, local * devices)
    blocks = lax.axis_size("ctx")
    cores = [list(range(core, blocks, 2)) for core in range(2)]
    own = exchange(maps, "ctx", cores)
    own, query, inside, code, code_t = lax.optimization_barrier(
        (own, query, inside, code, code_t)
    )
    other = lax.ppermute(own, "ctx", [(i, i ^ 1) for i in range(blocks)])
    states = exchange(scan_call(own, other), "ctx", cores)
    hidden, sent = finish_call(
        states,
        query,
        inside,
        gate_in[0],
        residual_in[0],
        head_gain[None],
        post_gain[None],
        code_t,
        out_proj,
    )
    both = ("dp", "ctx")
    arrived = exchange(sent.reshape(devices, local * SPAN, WIDTH), both)
    results = expert_call(arrived.reshape(sent.shape), expert_in, expert_out)
    returned = exchange(results.reshape(devices, local * SPAN, WIDTH), both)
    return combine_call(code, returned.reshape(sent.shape), hidden, local)[None]


def solution(mesh):
    tokens = P("dp", "ctx", None)
    heads = P("dp", None, "ctx")
    experts = P(("dp", "ctx"), None, None)
    in_specs = (tokens,) * 5 + (heads, heads, P("dp", None), P(), P(), P())
    in_specs += (experts, experts, tokens, tokens)
    return jax.shard_map(
        per_device, mesh=mesh, in_specs=in_specs, out_specs=tokens, check_vma=False
    )
```
